256 devices in a mesh: wave: 16 (over z, core), col: 16 (over x, y).
Axes of the slice: x: 4, y: 4, z: 8, core: 2. Of those that a mesh axis runs over, the one named last changes fastest.
Arguments:
- divergence: float32 [256, 2, 128, 1024], P('wave', None, 'col'), may hold values from -6 to 6
- analysis: float32 [128, 128], replicated, may hold values from -0.5 to 0.5
- synthesis: float32 [128, 128], replicated, may hold values from -0.5 to 0.5
- helmholtz: float32 [128], replicated, may hold values from 3e-07 to 0.0003
- legendre: bfloat16 [256, 1024, 1024], P('wave', None, 'col'), may hold values from -0.1875 to 0.1875
- wavenumbers: int32 [256], replicated, may hold values from 0 to 1023, as said below
- cycle_points: int32 [1024], replicated, may hold values from 2048 to 4096, as said below
Outputs:
- grid_field: bfloat16 [16, 64, 4096, 128], P('col', 'wave')
The draws below stay inside these ranges and needn't reach their ends.
Inputs may be any that keep to these rules, and one draw needn't show every extreme that they name: Distinct values; slots 2 i and 2 i + 1 hold two wavenumbers that add up to 1023. `cycle_points`: multiples of 16.
All inputs are finite; a program needn't handle non-finite values.
Results may differ from the reference program's by a relative error of at most 0.0062.
Values may be sent and summed in bfloat16 or wider, within the bound.
A program may use at most 64 MiB of HBM per device.

```python
import math
import jax
import jax.numpy as jnp
from jax import lax

L = 128
NN = 1024
LAT_DEV = 64
LON = 4096
M = 256
LAT = 1024
BLOCKS = 16


def draw_wavenumbers(key, part):
    key = jax.random.fold_in(key, 11)
    first_key, second_key = jax.random.split(key)
    half_count = M // 2
    others = jax.random.permutation(first_key, NN // 2 - 2)[:half_count - 2].astype(jnp.int32) + 2
    lower = jnp.concatenate([jnp.array([0, 1], dtype=jnp.int32), others])
    lower = jax.random.permutation(second_key, lower).astype(jnp.int32)
    paired = jnp.stack([lower, NN - 1 - lower], axis=1).reshape(M)
    return paired.astype(jnp.int32)


def draw_cycle_points(key, part):
    key = jax.random.fold_in(key, 23)
    first_key, second_key = jax.random.split(key)
    reductions = jax.random.randint(first_key, (LAT,), 0, LON // 32 + 1)
    counts = LON - 16 * reductions
    order = jax.random.permutation(second_key, LAT)
    counts = counts.at[order[0]].set(LON).at[order[1]].set(LON // 2)
    return counts.astype(jnp.int32)


def block_levels(key, shape, shards, least, largest):
    gain, own = 1.0, jax.random.fold_in(key, 6)
    for dim, blocks in shards:
        heights = jnp.exp(jax.random.uniform(jax.random.fold_in(own, dim), (blocks,), jnp.float32, least / len(shards), largest / len(shards)))
        gain = gain * jnp.repeat(heights, shape[dim] // blocks).reshape([-1 if axis == dim else 1 for axis in range(len(shape))])
    return gain


def centred(own_key, extent, scale, reach, shards=(), kind=jnp.bfloat16):
    factor_of = block_levels(own_key, extent, shards, -0.22, 0.18) if shards else 1.0
    entries = jax.random.normal(own_key, extent, jnp.float32) * scale * factor_of
    return jnp.minimum(jnp.maximum(entries, -reach), reach).astype(kind)


def setup_inputs(seed: int = 0) -> dict:
    key_list = jax.random.split(jax.random.key(seed), 8)
    return {
        "divergence": centred(key_list[0], (M, 2, L, NN), 1.0, 6.0, ((0, 16), (2, 16)), jnp.float32),
        "analysis": centred(key_list[1], (L, L), L ** -0.5, 0.5, (), jnp.float32),
        "synthesis": centred(key_list[2], (L, L), L ** -0.5, 0.5, (), jnp.float32),
        "helmholtz": jnp.clip(jnp.exp(jax.random.uniform(key_list[3], (L,), jnp.float32, math.log(3.000000106112566e-07), math.log(0.0003))), 3.000000106112566e-07, 0.0003),
        "legendre": centred(key_list[4], (M, NN, LAT), NN ** -0.5, 0.1875, ((0, 16), (2, 16))),
        "wavenumbers": draw_wavenumbers(jax.random.fold_in(key_list[7], 71), 0),
        "cycle_points": draw_cycle_points(jax.random.fold_in(key_list[7], 71), 0),
    }


def vertical(block, analysis, synthesis, helmholtz):
    count = block.shape[3]
    degree = jnp.arange(count, dtype=jnp.int32).astype(jnp.float32)
    factor = 1.0 / (1.0 + helmholtz[:, None] * (degree * (degree + 1.0))[None, :])
    modes = jnp.einsum('kl,srln->srkn', analysis, block, precision=lax.Precision.HIGHEST)
    return jnp.einsum('lk,srkn->srln', synthesis, modes * factor[None, None], precision=lax.Precision.HIGHEST)

def cycle_basis(wavenumbers, point_count, length, window):
    span = 64
    coarse_index = jnp.arange(length // span, dtype=jnp.int32) * span
    fine_index = jnp.arange(span, dtype=jnp.int32)
    scale = 2.0 * math.pi / point_count.astype(jnp.float32)
    coarse_angle = (coarse_index[:, None] * wavenumbers[None, :] % point_count).astype(jnp.float32) * scale
    fine_angle = (fine_index[:, None] * wavenumbers[None, :] % point_count).astype(jnp.float32) * scale
    coarse_cos, coarse_sin = (jnp.cos(coarse_angle), jnp.sin(coarse_angle))
    fine_cos, fine_sin = (jnp.cos(fine_angle), jnp.sin(fine_angle))
    cosine = coarse_cos[:, None, :] * fine_cos[None, :, :] - coarse_sin[:, None, :] * fine_sin[None, :, :]
    sine = coarse_sin[:, None, :] * fine_cos[None, :, :] + coarse_cos[:, None, :] * fine_sin[None, :, :]
    cosine = cosine.reshape(length, wavenumbers.shape[0])
    sine = sine.reshape(length, wavenumbers.shape[0])
    column = jnp.arange(length, dtype=jnp.int32)
    weight = jnp.where(wavenumbers == 0, 1.0, 2.0).astype(jnp.float32) / math.sqrt(window)
    valid = column[:, None] < point_count
    cosine = jnp.where(valid, weight[None, :] * cosine, 0.0)
    sine = jnp.where(valid, -weight[None, :] * sine, 0.0)
    return jnp.stack([cosine, sine], axis=2).reshape(length, 2 * wavenumbers.shape[0]).astype(jnp.bfloat16)

def reference(divergence, analysis, synthesis, helmholtz, legendre, wavenumbers, cycle_points):
    solved = vertical(divergence, analysis, synthesis, helmholtz)
    degree_index = jnp.arange(NN, dtype=jnp.int32)
    keep = degree_index[None, :] >= wavenumbers[:, None]
    coefs = jnp.where(keep[:, None, None, :], solved, 0.0).astype(jnp.bfloat16)

    def transform(pair):
        slot_block, slot_table = pair
        flat = slot_block.reshape(2 * L, NN)
        product = jnp.dot(slot_table.T, flat.T, preferred_element_type=jnp.float32)
        return product.reshape(LAT, 2, L).astype(jnp.bfloat16)
    field = lax.map(transform, (coefs, legendre))

    def synthesize(latitude):
        point_count = lax.dynamic_index_in_dim(cycle_points, latitude, 0, keepdims=False)
        basis = cycle_basis(wavenumbers, point_count, LON, M)
        values = lax.dynamic_index_in_dim(field, latitude, 1, keepdims=False).reshape(2 * M, L)
        return jnp.dot(basis, values, preferred_element_type=jnp.float32).astype(jnp.bfloat16)
    grid = lax.map(synthesize, jnp.arange(LAT, dtype=jnp.int32))
    return grid.reshape(BLOCKS, LAT_DEV, LON, L)
```

```python
import math

import jax
import jax.numpy as jnp
from jax import lax
from jax.experimental import pallas as pl
from jax.experimental.pallas import tpu as pltpu
from jax.sharding import PartitionSpec as P

MESH = pl.DeviceIdType.MESH
F32 = jnp.float32
BF16 = jnp.bfloat16
LON = 4096
WAVES = 16
SIDE = 4
ROUNDS = 4
MIB = 1 << 20


def iota(shape, dim):
    return lax.broadcasted_iota(jnp.int32, shape, dim)


def dot(a, b):
    return jnp.dot(a, b, preferred_element_type=F32)


def cos_sin(turn):
    quadrant = jnp.floor(turn + 0.5)
    x = (turn - quadrant) * (0.5 * math.pi)
    z = x * x
    s = x * (1.0 + z * (-1.0 / 6 + z * (1.0 / 120 + z * (-1.0 / 5040 + z * (1.0 / 362880)))))
    c = 1.0 + z * (-0.5 + z * (1.0 / 24 + z * (-1.0 / 720 + z * (1.0 / 40320))))
    odd = (quadrant == 1.0) | (quadrant == 3.0)
    cosine = jnp.where(odd, s, c)
    sine = jnp.where(odd, c, s)
    cosine = jnp.where((quadrant == 1.0) | (quadrant == 2.0), -cosine, cosine)
    sine = jnp.where((quadrant == 2.0) | (quadrant == 3.0), -sine, sine)
    return cosine, sine


def kernel(
    wn_s, cp_s, wn_v, div, analysis, synthesis, helm, leg_hbm, out_hbm,
    X, XE, leg, LP, AH, AL, SS, HM, C, CE, G32, G, F, ML, UA, VA, CB, SB, basis, acc, stage,
    p1_send, p1_recv, p2_send, p2_recv, xe_send, xe_recv, z_send, z_recv, leg_sem, out_sem,
):
    w = lax.axis_index("wave")
    col = lax.axis_index("col")
    cx, cy = col // SIDE, col % SIDE

    def wrap(v, n=SIDE):
        return lax.rem(v + n, n)

    first = (cx, cy)
    second = (cy, cx)

    def column(kind, d1, d2):
        return d1 * SIDE + d2 if kind == 0 else d2 * SIDE + d1

    def step_first(kind, by):
        return (w, column(kind, wrap(first[kind] + by), second[kind]))

    def step_second(kind, by):
        return (w, column(kind, first[kind], wrap(second[kind] + by)))

    barrier = pltpu.get_barrier_semaphore()
    for kind in range(2):
        for by in (-1, 1):
            pl.semaphore_signal(barrier, inc=1, device_id=step_first(kind, by), device_id_type=MESH)

    def greet(d, _):
        pl.semaphore_signal(
            barrier, inc=1, device_id=(lax.rem(w + d, WAVES), col), device_id_type=MESH
        )
        return 0

    lax.fori_loop(1, WAVES, greet, 0)
    leg_copy = pltpu.make_async_copy(leg_hbm, leg, leg_sem)
    leg_copy.start()

    def low_of(i):
        m = wn_s[w * 16 + 2 * i]
        return jnp.minimum(m, 1023 - m), jnp.where(m > 511, 1, 0)

    lanes = iota((16, 512), 1)
    tile_lane = iota((16, 128), 1)
    extra = jnp.zeros((16, 128), F32)
    for i in range(8):
        lo, swap = low_of(i)
        low = div[2 * i + swap].reshape(16, 1024)
        high = div[2 * i + 1 - swap].reshape(16, 1024)
        rolled = pltpu.roll(high[:, 512:], lo, 1)
        kind, rho = i % 2, i // 2
        own = X.at[kind, rho, second[kind], first[kind]]
        own[0] = jnp.where(lanes >= lo, low[:, :512], rolled).astype(BF16)
        own[1] = low[:, 512:].astype(BF16)
        moved = pltpu.roll(rolled[:, 384:], i + 1, 1)
        extra = jnp.where(tile_lane == i, moved, extra)
    XE[cy, cx] = extra.astype(BF16)

    pl.semaphore_wait(barrier, 4 + WAVES - 1)

    BULKS = ((0, 1), (1, 3))

    def send(src, dst, to, send_sem, recv_sem):
        return pltpu.make_async_remote_copy(
            src_ref=src, dst_ref=dst, send_sem=send_sem, recv_sem=recv_sem,
            device_id=to, device_id_type=MESH,
        )

    def p1(kind, bulk, which):
        at, size = BULKS[bulk]
        rs = pl.ds(at, size)
        d1, d2 = first[kind], second[kind]
        if which < 2:
            ref = X.at[kind, rs, d2, d1]
        elif which == 2:
            ref = X.at[kind, rs, d2, wrap(d1 - 1), 0]
        else:
            ref = X.at[kind, rs, d2, wrap(d1 + 1), 1]
        to = step_first(kind, 1 if which % 2 == 0 else -1)
        return send(ref, ref, to, p1_send.at[kind, bulk, which], p1_recv.at[kind, bulk, which])

    def p1_arrived(kind, bulk, which):
        at, size = BULKS[bulk]
        rs = pl.ds(at, size)
        d1, d2 = first[kind], second[kind]
        by = -1 if which % 2 == 0 else 1
        if which < 2:
            ref = X.at[kind, rs, d2, wrap(d1 + by)]
        else:
            ref = X.at[kind, rs, d2, wrap(d1 + 2), which - 2]
        send(ref, ref, step_first(kind, by), p1_send.at[kind, bulk, which],
             p1_recv.at[kind, bulk, which]).wait_recv()

    def p2(kind, rho, which):
        d2 = second[kind]
        if which < 2:
            ref = X.at[kind, rho, d2]
        elif which == 2:
            ref = X.at[kind, rho, wrap(d2 - 1), :, 0]
        else:
            ref = X.at[kind, rho, wrap(d2 + 1), :, 1]
        to = step_second(kind, 1 if which % 2 == 0 else -1)
        return send(ref, ref, to, p2_send.at[kind, rho, which], p2_recv.at[kind, rho, which])

    def p2_arrived(kind, rho, which):
        d2 = second[kind]
        by = -1 if which % 2 == 0 else 1
        if which < 2:
            ref = X.at[kind, rho, wrap(d2 + by)]
        else:
            ref = X.at[kind, rho, wrap(d2 + 2), :, which - 2]
        send(ref, ref, step_second(kind, by), p2_send.at[kind, rho, which],
             p2_recv.at[kind, rho, which]).wait_recv()

    def xe(which):
        ref = (XE.at[cy, cx], XE.at[cy, cx], XE.at[cy, wrap(cx - 1)],
               XE.at[cy], XE.at[cy], XE.at[wrap(cy - 1)])[which]
        by = -1 if which in (1, 4) else 1
        to = step_first(0, by) if which < 3 else step_second(0, by)
        return send(ref, ref, to, xe_send.at[which], xe_recv.at[which])

    def xe_arrived(which):
        ref = (XE.at[cy, wrap(cx - 1)], XE.at[cy, wrap(cx + 1)], XE.at[cy, wrap(cx + 2)],
               XE.at[wrap(cy - 1)], XE.at[wrap(cy + 1)], XE.at[wrap(cy + 2)])[which]
        by = 1 if which in (1, 4) else -1
        to = step_first(0, by) if which < 3 else step_second(0, by)
        send(ref, ref, to, xe_send.at[which], xe_recv.at[which]).wait_recv()

    for bulk in range(2):
        for which in range(2):
            for kind in range(2):
                p1(kind, bulk, which).start()
        if bulk == 0:
            xe(0).start()
            xe(1).start()

    a_full = analysis[...]
    a_hi = a_full.astype(BF16)
    a_lo = (a_full - a_hi.astype(F32)).astype(BF16)
    row = iota((128, 256), 0)
    j = iota((128, 256), 1)
    j2, j1 = j >> 6, (j >> 4) & 3
    for kind in range(2):
        level = (j1 * SIDE + j2 if kind == 0 else j2 * SIDE + j1) * 8 + (j & 7)
        for r in range(2):
            pick = jnp.where((row == level) & (((j >> 3) & 1) == r), 1.0, 0.0).astype(BF16)
            AH[kind, r * 128:(r + 1) * 128] = dot(a_hi, pick).astype(BF16)
            AL[kind, r * 128:(r + 1) * 128] = dot(a_lo, pick).astype(BF16)
    s_full = synthesis[...]
    s_hi = s_full.astype(BF16)
    SS[:, 0:128] = s_hi
    SS[:, 128:256] = (s_full - s_hi.astype(F32)).astype(BF16)
    h_rows = jnp.broadcast_to(helm[...], (128, 128)).T
    for q in range(4):
        HM[:, q * 128:(q + 1) * 128] = h_rows

    lane = iota((256, 512), 1)
    slot = ((lane >> 3) & 15) * 16 + 4 * (lane >> 7) + 2 * ((lane >> 1) & 1)
    choose = jnp.where(iota((256, 512), 0) == slot, 1.0, 0.0).astype(BF16)
    wn = jnp.broadcast_to(wn_v[...], (16, 256))
    upper = dot((wn >> 5).astype(F32).astype(BF16), choose)
    lower = dot((wn & 31).astype(F32).astype(BF16), choose)
    m0 = (upper * 32.0 + lower)[0:8]
    m_lo = jnp.minimum(m0, 1023.0 - m0)
    ML[...] = jnp.where((iota((8, 512), 1) & 1) == 1, 1023.0 - m_lo, m_lo)

    for kind in range(2):
        for which in range(2):
            p1_arrived(kind, 0, which)
            p1(kind, 0, 2 + which).start()
    xe_arrived(0)
    xe(2).start()
    xe_arrived(1)

    leg_copy.wait()

    def leg_pack(i, _):
        lo, swap = low_of(i)
        low = leg.at[2 * i + swap]
        high = leg.at[2 * i + 1 - swap]
        p = iota((64, 512), 1)
        rolled = pltpu.roll(high[:, 512:].astype(F32), lo, 1)
        LP[i, 0:64, 0:512] = jnp.where(p >= lo, low[:, 0:512].astype(F32), 0.0).astype(BF16)
        LP[i, 64:128, 0:512] = jnp.where(p < lo, rolled, 0.0).astype(BF16)
        LP[i, 0:64, 512:1024] = low[:, 512:]
        LP[i, 64:128, 512:1024] = jnp.zeros((64, 512), BF16)
        LP[i, 0:64, 1024:1152] = jnp.zeros((64, 128), BF16)
        moved = pltpu.roll(rolled[:, 384:], i + 1, 1)
        LP[i, 64:128, 1024:1152] = jnp.where(iota((64, 128), 1) == i, moved, 0.0).astype(BF16)
        return 0

    for kind in range(2):
        for which in range(2):
            p1_arrived(kind, 0, 2 + which)
    for which in range(2):
        for kind in range(2):
            p2(kind, 0, which).start()
    for kind in range(2):
        for which in range(2):
            p1_arrived(kind, 1, which)
            p1(kind, 1, 2 + which).start()
    lax.fori_loop(0, 4, leg_pack, 0)
    xe_arrived(2)
    xe(3).start()
    xe(4).start()
    for kind in range(2):
        for which in range(2):
            p1_arrived(kind, 1, 2 + which)
    for which in range(2):
        for kind in range(2):
            p2(kind, 1, which).start()
    xe_arrived(3)
    xe(5).start()
    lax.fori_loop(4, 8, leg_pack, 0)

    def make_angles(u):
        latitude = col * 64 + w * 4 + u
        points = jnp.full((64, 512), cp_s[latitude], jnp.int32).astype(F32)
        inverse = 1.0 / points
        m = jnp.broadcast_to(ML[0:1], (64, 512))
        index = iota((64, 512), 0).astype(F32)
        lane = iota((64, 512), 1)
        imaginary = ((lane >> 2) & 1) == 1
        weight = jnp.where(m == 0.0, 1.0, 2.0) / math.sqrt(256.0)

        def angle(product):
            rest = product - jnp.floor(product * inverse) * points
            rest = jnp.where(rest < 0.0, rest + points, rest)
            rest = jnp.where(rest >= points, rest - points, rest)
            return cos_sin(rest * (4.0 * inverse))

        c, s = angle(index * 64.0 * m)
        c, s = weight * c, -weight * s
        UA[...] = jnp.where(imaginary, s, c)
        VA[...] = jnp.where(imaginary, -c, s)
        c, s = angle(index * m)
        CB[...] = c
        SB[...] = s

    def make_basis(u):
        def rows(a8, _):
            some = pl.ds(pl.multiple_of(a8 * 8, 8), 8)
            for q in range(4):
                at = pl.ds(q * 128, 128)
                ua, va, cb, sb = UA[some, at], VA[some, at], CB[:, at], SB[:, at]
                for k in range(8):
                    value = ua[k:k + 1] * cb + va[k:k + 1] * sb
                    start = pl.multiple_of(a8 * 512, 512) + k * 64
                    basis[u, pl.ds(start, 64), at] = value.astype(BF16)
            return 0

        lax.fori_loop(0, 8, rows, 0)

    def solve(x, kind, n, count):
        modes = dot(AH[kind], x) + dot(AL[kind], x)
        factor = 1.0 / (1.0 + HM[:, 0:count] * (n * (n + 1.0)))
        out = []
        for r in range(2):
            part = modes[r * 128:(r + 1) * 128] * factor
            hi = part.astype(BF16)
            lo = (part - hi.astype(F32)).astype(BF16)
            both = jnp.concatenate([hi, hi], axis=0)
            out.append((dot(SS[...], both) + dot(SS[:, 0:128], lo)).astype(BF16))
        return out

    def field(kind, rho):
        i = 2 * rho + kind
        lo, _ = low_of(i)
        for h in range(2):
            p = iota((1, 512), 1) + h * 512
            n = jnp.where(p >= lo, p, p + 1024 - lo).astype(F32)
            x = X[kind, rho, :, :, h].reshape(256, 512)
            out = solve(x, kind, n, 512)
            for r in range(2):
                C[r * 128:(r + 1) * 128, h * 512:(h + 1) * 512] = out[r]
        contract = (((1,), (1,)), ((), ()))
        total = lax.dot_general(LP[i, :, 0:1024], C[...], contract, preferred_element_type=F32)
        total += lax.dot_general(LP[i, :, 1024:1152], CE[...], contract, preferred_element_type=F32)
        for r in range(2):
            for side in range(2):
                G32[pl.ds(r * 4 + kind * 2 + side, 64, stride=8)] = (
                    total[side * 64:(side + 1) * 64, r * 128:(r + 1) * 128]
                )

    def z_copy(rho, d):
        to = lax.rem(w + d, WAVES)
        return send(G.at[rho, to], F.at[rho, w], (to, col), z_send.at[rho, d], z_recv.at[rho, d])

    def z_start(rho):
        G[rho] = G32[...].reshape(WAVES, 2, 16, 128).astype(BF16)

        def one(d, _):
            z_copy(rho, d).start()
            return 0

        lax.fori_loop(1, WAVES, one, 0)
        F[rho, w] = G[rho, w]

    def z_wait(rho):
        def one(d, _):
            come = lax.rem(w - d + WAVES, WAVES)
            send(G.at[rho, come], F.at[rho, come], (come, col), z_send.at[rho, d],
                 z_recv.at[rho, d]).wait_recv()
            return 0

        lax.fori_loop(1, WAVES, one, 0)

    def grid(u, g):
        parts = []
        for rho in (2 * g, 2 * g + 1):
            tiles = F[rho, :, u // 2].astype(F32)
            at = (u % 2) * 8
            parts.append(tiles[:, at:at + 8].reshape(128, 128))
        values = jnp.concatenate(parts, axis=0).astype(BF16)
        points = cp_s[col * 64 + w * 4 + u]

        def rows(k, _):
            at = pl.ds(pl.multiple_of(k * 512, 512), 512)
            part = dot(basis[u, at, g * 256:(g + 1) * 256], values)
            if g == 0:
                acc[u, at] = part
            else:
                live = iota((512, 128), 0) + k * 512 < points
                stage[u, at] = jnp.where(live, acc[u, at] + part, 0.0).astype(BF16)
            return 0

        lax.fori_loop(0, LON // 512, rows, 0)

    def out_copy(u):
        return pltpu.make_async_copy(stage.at[u], out_hbm.at[0, u], out_sem.at[u])

    for rho in range(ROUNDS):
        for kind in range(2):
            for which in range(2):
                p2_arrived(kind, rho, which)
                p2(kind, rho, 2 + which).start()
        if rho < 2:
            for which in range(2):
                for kind in range(2):
                    p2(kind, rho + 2, which).start()
        if rho < 2:
            for u in (2 * rho, 2 * rho + 1):
                make_angles(u)
                make_basis(u)
        else:
            if rho == 2:
                z_wait(0)
                z_wait(1)
            for u in (2 * rho - 4, 2 * rho - 3):
                grid(u, 0)
        if rho == 0:
            xe_arrived(4)
            xe_arrived(5)
            n = jnp.zeros((1, 128), F32)
            for i in range(8):
                lo, _ = low_of(i)
                n = jnp.where(iota((1, 128), 1) == i, (1023 - lo).astype(F32), n)
            out = solve(XE[...].reshape(256, 128), 0, n, 128)
            for r in range(2):
                CE[r * 128:(r + 1) * 128] = out[r]
        for kind in range(2):
            for which in range(2):
                p2_arrived(kind, rho, 2 + which)
            field(kind, rho)
        z_start(rho)

    for kind in range(2):
        for which in range(4):
            for bulk in range(2):
                p1(kind, bulk, which).wait_send()
            for rho in range(ROUNDS):
                p2(kind, rho, which).wait_send()
    for which in range(6):
        xe(which).wait_send()
    z_wait(2)
    z_wait(3)
    for u in range(4):
        grid(u, 1)
        out_copy(u).start()
    for rho in range(ROUNDS):
        def sent(d, _, rho=rho):
            z_copy(rho, d).wait_send()
            return 0

        lax.fori_loop(1, WAVES, sent, 0)
    for u in range(4):
        out_copy(u).wait()


def on_device(divergence, analysis, synthesis, helmholtz, legendre, wavenumbers, cycle_points):
    vmem = pl.BlockSpec(memory_space=pltpu.VMEM)
    smem = pl.BlockSpec(memory_space=pltpu.SMEM)
    hbm = pl.BlockSpec(memory_space=pl.ANY)
    dma = pltpu.SemaphoreType.DMA
    return pl.pallas_call(
        kernel,
        out_shape=jax.ShapeDtypeStruct((1, 4, LON, 128), BF16),
        in_specs=[smem, smem, vmem, vmem, vmem, vmem, vmem, hbm],
        out_specs=hbm,
        scratch_shapes=[
            pltpu.VMEM((2, ROUNDS, SIDE, SIDE, 2, 16, 512), BF16),
            pltpu.VMEM((SIDE, SIDE, 16, 128), BF16),
            pltpu.VMEM((16, 64, 1024), BF16),
            pltpu.VMEM((8, 128, 1152), BF16),
            pltpu.VMEM((2, 256, 256), BF16),
            pltpu.VMEM((2, 256, 256), BF16),
            pltpu.VMEM((128, 256), BF16),
            pltpu.VMEM((128, 512), F32),
            pltpu.VMEM((256, 1024), BF16),
            pltpu.VMEM((256, 128), BF16),
            pltpu.VMEM((512, 128), F32),
            pltpu.VMEM((ROUNDS, WAVES, 2, 16, 128), BF16),
            pltpu.VMEM((ROUNDS, WAVES, 2, 16, 128), BF16),
            pltpu.VMEM((8, 512), F32),
            pltpu.VMEM((64, 512), F32),
            pltpu.VMEM((64, 512), F32),
            pltpu.VMEM((64, 512), F32),
            pltpu.VMEM((64, 512), F32),
            pltpu.VMEM((4, LON, 512), BF16),
            pltpu.VMEM((4, LON, 128), F32),
            pltpu.VMEM((4, LON, 128), BF16),
            dma((2, 2, 4)), dma((2, 2, 4)),
            dma((2, ROUNDS, 4)), dma((2, ROUNDS, 4)),
            dma((6,)), dma((6,)),
            dma((ROUNDS, WAVES)), dma((ROUNDS, WAVES)),
            dma(()), dma((4,)),
        ],
        compiler_params=pltpu.CompilerParams(
            collective_id=0, has_side_effects=True, vmem_limit_bytes=58 * MIB
        ),
        cost_estimate=pl.CostEstimate(flops=6 << 30, bytes_accessed=8 * MIB, transcendentals=0),
    )(
        wavenumbers, cycle_points, wavenumbers.reshape(1, 256), divergence, analysis, synthesis,
        helmholtz.reshape(1, 128), jnp.swapaxes(legendre, 1, 2),
    )


def solution(mesh):
    placed = (P("wave", None, "col", None), P(), P(), P(), P("wave", None, "col"), P(), P())
    return jax.shard_map(
        on_device,
        mesh=mesh,
        in_specs=placed,
        out_specs=P("col", "wave", None, None),
        check_vma=False,
    )
```

```python
import math

import jax
import jax.numpy as jnp
from jax import lax
from jax.experimental import pallas as pl
from jax.experimental.pallas import tpu as pltpu
from jax.sharding import PartitionSpec as P

MESH = pl.DeviceIdType.MESH
F32 = jnp.float32
BF16 = jnp.bfloat16
LON = 4096
WAVES = 16
HALF = LON // 2
SIDE = 4
ROUNDS = 4
BEFORE = 2
MIB = 1 << 20


def iota(shape, dim):
    return lax.broadcasted_iota(jnp.int32, shape, dim)


def dot(a, b):
    return jnp.dot(a, b, preferred_element_type=F32)


def cos_sin(turn):
    quadrant = jnp.floor(turn + 0.5)
    x = (turn - quadrant) * (0.5 * math.pi)
    z = x * x
    s = x * (1.0 + z * (-1.0 / 6 + z * (1.0 / 120 + z * (-1.0 / 5040 + z * (1.0 / 362880)))))
    c = 1.0 + z * (-0.5 + z * (1.0 / 24 + z * (-1.0 / 720 + z * (1.0 / 40320))))
    odd = (quadrant == 1.0) | (quadrant == 3.0)
    cosine = jnp.where(odd, s, c)
    sine = jnp.where(odd, c, s)
    cosine = jnp.where((quadrant == 1.0) | (quadrant == 2.0), -cosine, cosine)
    sine = jnp.where((quadrant == 2.0) | (quadrant == 3.0), -sine, sine)
    return cosine, sine


def gather_kernel(
    wn_s, cp_s, wn_v, div, analysis, synthesis, helm, leg_hbm, basis_hbm, values_hbm,
    X, XE, leg, LP, AHL, SS, HM, C, CE, G32, G, F, ML, SG, UA, VA, CB, SB, basis, V,
    p1_send, p1_recv, p2_send, p2_recv, xe_send, xe_recv, z_send, z_recv,
    leg_sem, basis_sem, values_sem,
):
    w = lax.axis_index("wave")
    col = lax.axis_index("col")
    cx, cy = col // SIDE, col % SIDE

    def wrap(v, n=SIDE):
        return lax.rem(v + n, n)

    first = (cx, cy)
    second = (cy, cx)

    def column(kind, d1, d2):
        return d1 * SIDE + d2 if kind == 0 else d2 * SIDE + d1

    def step_first(kind, by):
        return (w, column(kind, wrap(first[kind] + by), second[kind]))

    def step_second(kind, by):
        return (w, column(kind, first[kind], wrap(second[kind] + by)))

    barrier = pltpu.get_barrier_semaphore()
    for kind in range(2):
        for by in (1, 2, 3):
            pl.semaphore_signal(barrier, inc=1, device_id=step_first(kind, by), device_id_type=MESH)

    def greet(d, _):
        pl.semaphore_signal(
            barrier, inc=1, device_id=(lax.rem(w + d, WAVES), col), device_id_type=MESH
        )
        return 0

    lax.fori_loop(1, WAVES, greet, 0)
    leg_copy = pltpu.make_async_copy(leg_hbm, leg, leg_sem)
    leg_copy.start()

    def low_of(i):
        m = wn_s[w * 16 + 2 * i]
        return jnp.minimum(m, 1023 - m), jnp.where(m > 511, 1, 0)

    lanes = iota((16, 512), 1)
    tile_lane = iota((16, 128), 1)
    extra = jnp.zeros((16, 128), F32)
    for i in range(8):
        lo, swap = low_of(i)
        low = div[2 * i + swap].reshape(16, 1024)
        high = div[2 * i + 1 - swap].reshape(16, 1024)
        rolled = pltpu.roll(high[:, 512:], lo, 1)
        kind, rho = i % 2, i // 2
        own = X.at[kind, rho, second[kind], first[kind]]
        own[0] = jnp.where(lanes >= lo, low[:, :512], rolled).astype(BF16)
        own[1] = low[:, 512:].astype(BF16)
        moved = pltpu.roll(rolled[:, 384:], i + 1, 1)
        extra = jnp.where(tile_lane == i, moved, extra)
    XE[cy, cx] = extra.astype(BF16)

    a_full = analysis[...]
    a_hi = a_full.astype(BF16)
    a_lo = (a_full - a_hi.astype(F32)).astype(BF16)
    row = iota((128, 256), 0)
    j = iota((128, 256), 1)
    j2, j1 = j >> 6, (j >> 4) & 3
    for kind in range(2):
        level = (j1 * SIDE + j2 if kind == 0 else j2 * SIDE + j1) * 8 + (j & 7)
        for r in range(2):
            pick = jnp.where((row == level) & (((j >> 3) & 1) == r), 1.0, 0.0).astype(BF16)
            AHL[kind, r * 128:(r + 1) * 128] = dot(a_hi, pick).astype(BF16)
            AHL[kind, 256 + r * 128:256 + (r + 1) * 128] = dot(a_lo, pick).astype(BF16)
    s_full = synthesis[...]
    s_hi = s_full.astype(BF16)
    SS[:, 0:128] = s_hi
    SS[:, 128:256] = (s_full - s_hi.astype(F32)).astype(BF16)
    h_rows = jnp.broadcast_to(helm[...], (128, 128)).T
    for q in range(4):
        HM[:, q * 128:(q + 1) * 128] = h_rows

    lane = iota((256, 512), 1)
    slot = ((lane >> 3) & 15) * 16 + 4 * (lane >> 7) + 2 * ((lane >> 1) & 1)
    choose = jnp.where(iota((256, 512), 0) == slot, 1.0, 0.0).astype(BF16)
    wn = jnp.broadcast_to(wn_v[...], (16, 256))
    upper = dot((wn >> 5).astype(F32).astype(BF16), choose)
    lower = dot((wn & 31).astype(F32).astype(BF16), choose)
    m0 = (upper * 32.0 + lower)[0:8]
    m_lo = jnp.minimum(m0, 1023.0 - m0)
    m_lane = jnp.where((iota((8, 512), 1) & 1) == 1, 1023.0 - m_lo, m_lo)
    ML[...] = m_lane
    sign = 1.0 - 2.0 * (m_lane - 2.0 * jnp.floor(m_lane * 0.5))
    for q in range(4):
        part = jnp.broadcast_to(sign[0:1, q * 128:(q + 1) * 128], (128, 128))
        SG[q * 128:(q + 1) * 128] = part.T

    def make_angles(u):
        latitude = col * 64 + w * 4 + u

        def angle(index, count):
            points = jnp.full((count, 512), cp_s[latitude], jnp.int32).astype(F32)
            inverse = 1.0 / points
            product = index.astype(F32) * jnp.broadcast_to(ML[0:1], (count, 512))
            rest = product - jnp.floor(product * inverse) * points
            rest = jnp.where(rest < 0.0, rest + points, rest)
            rest = jnp.where(rest >= points, rest - points, rest)
            return cos_sin(rest * (4.0 * inverse))

        c, s = angle(iota((32, 512), 0) * 64, 32)
        weight = jnp.where(ML[0:1] == 0.0, 1.0, 2.0) / math.sqrt(256.0)
        imaginary = ((iota((32, 512), 1) >> 2) & 1) == 1
        c, s = weight * c, -weight * s
        UA[...] = jnp.where(imaginary, s, c)
        VA[...] = jnp.where(imaginary, -c, s)
        c, s = angle(iota((64, 512), 0), 64)
        CB[...] = c
        SB[...] = s

    def basis_copy(u):
        return pltpu.make_async_copy(basis.at[u], basis_hbm.at[u], basis_sem.at[u])

    def make_basis(u, _):
        make_angles(u)

        def rows(a8, _):
            some = pl.ds(pl.multiple_of(a8 * 8, 8), 8)
            for q in range(4):
                at = pl.ds(q * 128, 128)
                ua, va, cb, sb = UA[some, at], VA[some, at], CB[:, at], SB[:, at]
                for k in range(8):
                    value = ua[k:k + 1] * cb + va[k:k + 1] * sb
                    start = pl.multiple_of(a8 * 512, 512) + k * 64
                    basis[u, pl.ds(start, 64), at] = value.astype(BF16)
            return 0

        lax.fori_loop(0, HALF // 512, rows, 0)
        basis_copy(u).start()
        return 0

    lax.fori_loop(0, BEFORE, make_basis, 0)
    pl.semaphore_wait(barrier, 6 + WAVES - 1)

    BULKS = ((0, 1), (1, 1), (2, 2))

    def send(src, dst, to, send_sem, recv_sem):
        return pltpu.make_async_remote_copy(
            src_ref=src, dst_ref=dst, send_sem=send_sem, recv_sem=recv_sem,
            device_id=to, device_id_type=MESH,
        )

    def bytes_of(ref, send_sem, recv_sem):
        return send(ref, ref, step_first(0, 1), send_sem, recv_sem)

    def p1_start(kind, bulk):
        at, size = BULKS[bulk]
        ref = X.at[kind, pl.ds(at, size), second[kind], first[kind]]
        for by in (2, 1, 3):
            send(ref, ref, step_first(kind, by), p1_send.at[kind, bulk], p1_recv.at[kind, bulk]).start()

    def p1_all(kind, bulk):
        at, size = BULKS[bulk]
        ref = X.at[kind, pl.ds(at, size), second[kind], pl.ds(0, 3)]
        return bytes_of(ref, p1_send.at[kind, bulk], p1_recv.at[kind, bulk])

    def p2(kind, rho, which):
        d2 = second[kind]
        if which < 2:
            ref = X.at[kind, rho, d2]
        elif which == 2:
            ref = X.at[kind, rho, wrap(d2 - 1), :, 0]
        else:
            ref = X.at[kind, rho, wrap(d2 + 1), :, 1]
        to = step_second(kind, 1 if which % 2 == 0 else -1)
        return send(ref, ref, to, p2_send.at[kind, rho], p2_recv.at[kind, rho, min(which, 2)])

    def p2_direct(rho):
        for which in range(2):
            for kind in range(2):
                p2(kind, rho, which).start()

    def p2_row(kind, rho, which):
        ref = X.at[kind, rho, wrap(second[kind] + (-1 if which == 0 else 1))]
        bytes_of(ref, p2_send.at[kind, rho], p2_recv.at[kind, rho, which]).wait_recv()

    def p2_relayed(kind, rho):
        ref = X.at[kind, rho, wrap(second[kind] + 2)]
        bytes_of(ref, p2_send.at[kind, rho], p2_recv.at[kind, rho, 2]).wait_recv()

    def xe_start(stage):
        ref = XE.at[cy, cx] if stage == 0 else XE.at[cy]
        for by in (2, 1, 3):
            to = step_first(0, by) if stage == 0 else step_second(0, by)
            send(ref, ref, to, xe_send.at[stage], xe_recv.at[stage]).start()

    def xe_all(stage):
        ref = XE.at[cy, pl.ds(0, 3)] if stage == 0 else XE.at[pl.ds(0, 3)]
        return bytes_of(ref, xe_send.at[stage], xe_recv.at[stage])

    for bulk in range(3):
        for kind in range(2):
            p1_start(kind, bulk)
        if bulk == 0:
            xe_start(0)

    lax.fori_loop(BEFORE, BEFORE + 1, make_basis, 0)
    leg_copy.wait()

    def leg_pack(i, _):
        lo, swap = low_of(i)
        low = leg.at[2 * i + swap]
        high = leg.at[2 * i + 1 - swap]
        p = iota((64, 512), 1)
        rolled = pltpu.roll(high[:, 512:].astype(F32), lo, 1)
        LP[i, 0:64, 0:512] = jnp.where(p >= lo, low[:, 0:512].astype(F32), 0.0).astype(BF16)
        LP[i, 64:128, 0:512] = jnp.where(p < lo, rolled, 0.0).astype(BF16)
        LP[i, 0:64, 512:1024] = low[:, 512:]
        LP[i, 64:128, 512:1024] = jnp.zeros((64, 512), BF16)
        LP[i, 0:64, 1024:1152] = jnp.zeros((64, 128), BF16)
        moved = pltpu.roll(rolled[:, 384:], i + 1, 1)
        LP[i, 64:128, 1024:1152] = jnp.where(iota((64, 128), 1) == i, moved, 0.0).astype(BF16)
        return 0

    for kind in range(2):
        p1_all(kind, 0).wait_recv()
    p2_direct(0)
    xe_all(0).wait_recv()
    xe_start(1)
    lax.fori_loop(0, 4, leg_pack, 0)
    for kind in range(2):
        p1_all(kind, 1).wait_recv()
    p2_direct(1)
    lax.fori_loop(4, 8, leg_pack, 0)
    for kind in range(2):
        p1_all(kind, 2).wait_recv()

    def solve(x, kind, n, count):
        modes = dot(AHL[kind], x)
        modes = modes[0:256] + modes[256:512]
        factor = 1.0 / (1.0 + HM[:, 0:count] * (n * (n + 1.0)))
        out = []
        for r in range(2):
            part = modes[r * 128:(r + 1) * 128] * factor
            hi = part.astype(BF16)
            lo = (part - hi.astype(F32)).astype(BF16)
            both = jnp.concatenate([hi, hi], axis=0)
            out.append((dot(SS[...], both) + dot(SS[:, 0:128], lo)).astype(BF16))
        return out

    def field(kind, rho):
        i = 2 * rho + kind
        lo, _ = low_of(i)
        for h in range(2):
            p = iota((1, 512), 1) + h * 512
            n = jnp.where(p >= lo, p, p + 1024 - lo).astype(F32)
            x = X[kind, rho, :, :, h].reshape(256, 512)
            out = solve(x, kind, n, 512)
            for r in range(2):
                C[r * 128:(r + 1) * 128, h * 512:(h + 1) * 512] = out[r]
        contract = (((1,), (1,)), ((), ()))
        total = lax.dot_general(LP[i, :, 0:1024], C[...], contract, preferred_element_type=F32)
        total += lax.dot_general(LP[i, :, 1024:1152], CE[...], contract, preferred_element_type=F32)
        for r in range(2):
            for side in range(2):
                G32[pl.ds(r * 4 + kind * 2 + side, 64, stride=8)] = (
                    total[side * 64:(side + 1) * 64, r * 128:(r + 1) * 128]
                )

    def z_start(rho):
        G[rho] = G32[...].reshape(WAVES, 2, 16, 128).astype(BF16)

        def one(d, _):
            to = lax.rem(w + d, WAVES)
            send(G.at[rho, to], F.at[rho, w], (to, col), z_send.at[rho], z_recv.at[rho]).start()
            return 0

        lax.fori_loop(1, WAVES, one, 0)
        F[rho, w] = G[rho, w]

    def z_all(rho):
        return bytes_of(F.at[rho, pl.ds(0, WAVES - 1)], z_send.at[rho], z_recv.at[rho])

    def values_copy(rho):
        return pltpu.make_async_copy(V.at[rho], values_hbm.at[rho], values_sem.at[rho])

    def make_values(rho):
        z_all(rho).wait_recv()
        sign = SG[rho * 128:(rho + 1) * 128]
        for u in range(4):
            tiles = F[rho, :, u // 2].astype(F32)
            at = (u % 2) * 8
            part = tiles[:, at:at + 8].reshape(128, 128)
            V[rho, u, :, 0:128] = part.astype(BF16)
            V[rho, u, :, 128:256] = (part * sign).astype(BF16)
        values_copy(rho).start()

    for rho in range(ROUNDS):
        for kind in range(2):
            for which in range(2):
                p2_row(kind, rho, which)
                p2(kind, rho, 2 + which).start()
        if rho < 2:
            p2_direct(rho + 2)
        if rho == 0:
            lax.fori_loop(BEFORE + 1, 4, make_basis, 0)
            xe_all(1).wait_recv()
            n = jnp.zeros((1, 128), F32)
            for i in range(8):
                lo, _ = low_of(i)
                n = jnp.where(iota((1, 128), 1) == i, (1023 - lo).astype(F32), n)
            out = solve(XE[...].reshape(256, 128), 0, n, 128)
            for r in range(2):
                CE[r * 128:(r + 1) * 128] = out[r]
        if rho >= 2:
            make_values(rho - 2)
        for kind in range(2):
            p2_relayed(kind, rho)
            field(kind, rho)
        z_start(rho)

    for kind in range(2):
        for bulk in range(3):
            p1_all(kind, bulk).wait_send()
        for rho in range(ROUNDS):
            ref = X.at[kind, rho, pl.ds(0, 3)]
            bytes_of(ref, p2_send.at[kind, rho], p2_recv.at[kind, rho, 0]).wait_send()
    for stage in range(2):
        xe_all(stage).wait_send()
    for u in range(4):
        basis_copy(u).wait()
    make_values(2)
    make_values(3)
    for rho in range(ROUNDS):
        z_all(rho).wait_send()
        values_copy(rho).wait()


def grid_kernel(cp_s, basis_hbm, values_hbm, out_hbm, basis, V, D, stage, basis_sem, values_sem, out_sem):
    first = lax.axis_index("col") * 64 + lax.axis_index("wave") * 4

    def basis_copy(u, b):
        at = pl.ds(b * 1024, 1024)
        return pltpu.make_async_copy(basis_hbm.at[u, at], basis.at[u, at], basis_sem.at[u, b])

    def values_copy(u):
        return pltpu.make_async_copy(values_hbm.at[:, u], V.at[u], values_sem.at[u])

    def out_copy(u, b):
        at = pl.ds(b * HALF, HALF)
        return pltpu.make_async_copy(stage.at[u, at], out_hbm.at[0, u, at], out_sem.at[u, b])

    for u in range(4):
        values_copy(u).start()
        for b in range(2):
            basis_copy(u, b).start()
    for u in range(4):
        points = cp_s[first + u]
        half = points >> 1
        values_copy(u).wait()
        values = V[u].reshape(512, 256)

        def turned(at):
            return D[pl.ds(pl.multiple_of(1024 + at - half, 8), 512)]

        for b in range(2):
            basis_copy(u, b).wait()
            both = dot(basis[u, b * 1024:(b + 1) * 1024], values)
            D[1024 + b * 1024:2048 + b * 1024] = both[:, 128:256]
            plus = both[:, 0:128]
            if b == 0:
                stage[u, 0:1024] = plus.astype(BF16)
            else:
                for k in range(2):
                    at = 1024 + k * 512
                    j = iota((512, 128), 0) + at
                    here = plus[k * 512:(k + 1) * 512]
                    stage[u, at:at + 512] = jnp.where(j < half, here, turned(at)).astype(BF16)
        out_copy(u, 0).start()
        for k in range(4):
            at = HALF + k * 512
            j = iota((512, 128), 0) + at
            stage[u, at:at + 512] = jnp.where(j < points, turned(at), 0.0).astype(BF16)
        out_copy(u, 1).start()
    for u in range(4):
        for b in range(2):
            out_copy(u, b).wait()


def on_device(divergence, analysis, synthesis, helmholtz, legendre, wavenumbers, cycle_points):
    vmem = pl.BlockSpec(memory_space=pltpu.VMEM)
    smem = pl.BlockSpec(memory_space=pltpu.SMEM)
    hbm = pl.BlockSpec(memory_space=pl.ANY)
    dma = pltpu.SemaphoreType.DMA
    basis, values = pl.pallas_call(
        gather_kernel,
        out_shape=(
            jax.ShapeDtypeStruct((4, HALF, 512), BF16),
            jax.ShapeDtypeStruct((ROUNDS, 4, 128, 256), BF16),
        ),
        in_specs=[smem, smem, vmem, vmem, vmem, vmem, vmem, hbm],
        out_specs=(hbm, hbm),
        scratch_shapes=[
            pltpu.VMEM((2, ROUNDS, SIDE, SIDE, 2, 16, 512), BF16),
            pltpu.VMEM((SIDE, SIDE, 16, 128), BF16),
            pltpu.VMEM((16, 64, 1024), BF16),
            pltpu.VMEM((8, 128, 1152), BF16),
            pltpu.VMEM((2, 512, 256), BF16),
            pltpu.VMEM((128, 256), BF16),
            pltpu.VMEM((128, 512), F32),
            pltpu.VMEM((256, 1024), BF16),
            pltpu.VMEM((256, 128), BF16),
            pltpu.VMEM((512, 128), F32),
            pltpu.VMEM((ROUNDS, WAVES, 2, 16, 128), BF16),
            pltpu.VMEM((ROUNDS, WAVES, 2, 16, 128), BF16),
            pltpu.VMEM((8, 512), F32),
            pltpu.VMEM((512, 128), F32),
            pltpu.VMEM((32, 512), F32),
            pltpu.VMEM((32, 512), F32),
            pltpu.VMEM((64, 512), F32),
            pltpu.VMEM((64, 512), F32),
            pltpu.VMEM((4, HALF, 512), BF16),
            pltpu.VMEM((ROUNDS, 4, 128, 256), BF16),
            dma((2, 3)), dma((2, 3)),
            dma((2, ROUNDS)), dma((2, ROUNDS, 3)),
            dma((2,)), dma((2,)),
            dma((ROUNDS,)), dma((ROUNDS,)),
            dma(()), dma((4,)), dma((ROUNDS,)),
        ],
        compiler_params=pltpu.CompilerParams(
            collective_id=0, has_side_effects=True, vmem_limit_bytes=48 * MIB
        ),
        cost_estimate=pl.CostEstimate(flops=4 << 30, bytes_accessed=12 * MIB, transcendentals=0),
    )(
        wavenumbers, cycle_points, wavenumbers.reshape(1, 256), divergence, analysis, synthesis,
        helmholtz.reshape(1, 128), jnp.swapaxes(legendre, 1, 2),
    )
    return pl.pallas_call(
        grid_kernel,
        out_shape=jax.ShapeDtypeStruct((1, 4, LON, 128), BF16),
        in_specs=[smem, hbm, hbm],
        out_specs=hbm,
        scratch_shapes=[
            pltpu.VMEM((4, HALF, 512), BF16),
            pltpu.VMEM((4, ROUNDS, 128, 256), BF16),
            pltpu.VMEM((LON, 128), F32),
            pltpu.VMEM((4, LON, 128), BF16),
            dma((4, 2)), dma((4,)), dma((4, 2)),
        ],
        compiler_params=pltpu.CompilerParams(vmem_limit_bytes=40 * MIB),
        cost_estimate=pl.CostEstimate(flops=4 << 30, bytes_accessed=13 * MIB, transcendentals=0),
    )(cycle_points, basis, values)


def solution(mesh):
    placed = (P("wave", None, "col", None), P(), P(), P(), P("wave", None, "col"), P(), P())
    return jax.shard_map(
        on_device,
        mesh=mesh,
        in_specs=placed,
        out_specs=P("col", "wave", None, None),
        check_vma=False,
    )
```

```python
import math

import jax
import jax.numpy as jnp
from jax import lax
from jax.experimental import pallas as pl
from jax.experimental.pallas import tpu as pltpu
from jax.sharding import PartitionSpec as P

MESH = pl.DeviceIdType.MESH
F32 = jnp.float32
BF16 = jnp.bfloat16
LON = 4096
WAVES = 16
HALF = LON // 2
SIDE = 4
ROUNDS = 4
BEFORE = 2
MIB = 1 << 20


def iota(shape, dim):
    return lax.broadcasted_iota(jnp.int32, shape, dim)


def dot(a, b):
    return jnp.dot(a, b, preferred_element_type=F32)


def cos_sin(turn):
    quadrant = jnp.floor(turn + 0.5)
    x = (turn - quadrant) * (0.5 * math.pi)
    z = x * x
    s = x * (1.0 + z * (-1.0 / 6 + z * (1.0 / 120 + z * (-1.0 / 5040 + z * (1.0 / 362880)))))
    c = 1.0 + z * (-0.5 + z * (1.0 / 24 + z * (-1.0 / 720 + z * (1.0 / 40320))))
    odd = (quadrant == 1.0) | (quadrant == 3.0)
    cosine = jnp.where(odd, s, c)
    sine = jnp.where(odd, c, s)
    cosine = jnp.where((quadrant == 1.0) | (quadrant == 2.0), -cosine, cosine)
    sine = jnp.where((quadrant == 2.0) | (quadrant == 3.0), -sine, sine)
    return cosine, sine


def gather_kernel(
    wn_s, cp_s, wn_v, div, analysis, synthesis, helm, leg_hbm, basis_hbm, values_hbm,
    X, XE, leg, LP, AHL, SS, HM, C, CE, G32, G, F, ML, SG, UA, VA, CB, SB, basis, V,
    p1_send, p1_recv, p2_send, p2_recv, xe_send, xe_recv, z_send, z_recv,
    leg_sem, basis_sem, values_sem,
):
    w = lax.axis_index("wave")
    col = lax.axis_index("col")
    cx, cy = col // SIDE, col % SIDE

    def wrap(v, n=SIDE):
        return lax.rem(v + n, n)

    first = (cx, cy)
    second = (cy, cx)

    def column(kind, d1, d2):
        return d1 * SIDE + d2 if kind == 0 else d2 * SIDE + d1

    def step_first(kind, by):
        return (w, column(kind, wrap(first[kind] + by), second[kind]))

    def step_second(kind, by):
        return (w, column(kind, first[kind], wrap(second[kind] + by)))

    barrier = pltpu.get_barrier_semaphore()
    for kind in range(2):
        for by in (1, 2, 3):
            pl.semaphore_signal(barrier, inc=1, device_id=step_first(kind, by), device_id_type=MESH)

    def greet(d, _):
        pl.semaphore_signal(
            barrier, inc=1, device_id=(lax.rem(w + d, WAVES), col), device_id_type=MESH
        )
        return 0

    lax.fori_loop(1, WAVES, greet, 0)
    leg_copy = pltpu.make_async_copy(leg_hbm, leg, leg_sem)
    leg_copy.start()

    def low_of(i):
        m = wn_s[w * 16 + 2 * i]
        return jnp.minimum(m, 1023 - m), jnp.where(m > 511, 1, 0)

    lanes = iota((16, 512), 1)
    tile_lane = iota((16, 128), 1)
    extra = jnp.zeros((16, 128), F32)
    for i in range(8):
        lo, swap = low_of(i)
        low = div[2 * i + swap].reshape(16, 1024)
        high = div[2 * i + 1 - swap].reshape(16, 1024)
        rolled = pltpu.roll(high[:, 512:], lo, 1)
        kind, rho = i % 2, i // 2
        own = X.at[kind, rho, second[kind], first[kind]]
        own[0] = jnp.where(lanes >= lo, low[:, :512], rolled).astype(BF16)
        own[1] = low[:, 512:].astype(BF16)
        moved = pltpu.roll(rolled[:, 384:], i + 1, 1)
        extra = jnp.where(tile_lane == i, moved, extra)
    XE[cy, cx] = extra.astype(BF16)

    a_full = analysis[...]
    a_hi = a_full.astype(BF16)
    a_lo = (a_full - a_hi.astype(F32)).astype(BF16)
    row = iota((128, 256), 0)
    j = iota((128, 256), 1)
    j2, j1 = j >> 6, (j >> 4) & 3
    for kind in range(2):
        level = (j1 * SIDE + j2 if kind == 0 else j2 * SIDE + j1) * 8 + (j & 7)
        for r in range(2):
            pick = jnp.where((row == level) & (((j >> 3) & 1) == r), 1.0, 0.0).astype(BF16)
            AHL[kind, r * 128:(r + 1) * 128] = dot(a_hi, pick).astype(BF16)
            AHL[kind, 256 + r * 128:256 + (r + 1) * 128] = dot(a_lo, pick).astype(BF16)
    s_full = synthesis[...]
    s_hi = s_full.astype(BF16)
    SS[:, 0:128] = s_hi
    SS[:, 128:256] = (s_full - s_hi.astype(F32)).astype(BF16)
    h_rows = jnp.broadcast_to(helm[...], (128, 128)).T
    for q in range(4):
        HM[:, q * 128:(q + 1) * 128] = h_rows

    lane = iota((256, 512), 1)
    slot = ((lane >> 3) & 15) * 16 + 4 * (lane >> 7) + 2 * ((lane >> 1) & 1)
    choose = jnp.where(iota((256, 512), 0) == slot, 1.0, 0.0).astype(BF16)
    wn = jnp.broadcast_to(wn_v[...], (16, 256))
    upper = dot((wn >> 5).astype(F32).astype(BF16), choose)
    lower = dot((wn & 31).astype(F32).astype(BF16), choose)
    m0 = (upper * 32.0 + lower)[0:8]
    m_lo = jnp.minimum(m0, 1023.0 - m0)
    m_lane = jnp.where((iota((8, 512), 1) & 1) == 1, 1023.0 - m_lo, m_lo)
    ML[...] = m_lane
    sign = 1.0 - 2.0 * (m_lane - 2.0 * jnp.floor(m_lane * 0.5))
    for q in range(4):
        part = jnp.broadcast_to(sign[0:1, q * 128:(q + 1) * 128], (128, 128))
        SG[q * 128:(q + 1) * 128] = part.T

    def make_angles(u):
        latitude = col * 64 + w * 4 + u

        def angle(index, count):
            points = jnp.full((count, 512), cp_s[latitude], jnp.int32).astype(F32)
            inverse = 1.0 / points
            product = index.astype(F32) * jnp.broadcast_to(ML[0:1], (count, 512))
            rest = product - jnp.floor(product * inverse) * points
            rest = jnp.where(rest < 0.0, rest + points, rest)
            rest = jnp.where(rest >= points, rest - points, rest)
            return cos_sin(rest * (4.0 * inverse))

        c, s = angle(iota((32, 512), 0) * 64, 32)
        weight = jnp.where(ML[0:1] == 0.0, 1.0, 2.0) / math.sqrt(256.0)
        imaginary = ((iota((32, 512), 1) >> 2) & 1) == 1
        c, s = weight * c, -weight * s
        UA[...] = jnp.where(imaginary, s, c)
        VA[...] = jnp.where(imaginary, -c, s)
        c, s = angle(iota((64, 512), 0), 64)
        CB[...] = c
        SB[...] = s

    def basis_copy(u):
        return pltpu.make_async_copy(basis.at[u], basis_hbm.at[u], basis_sem.at[u])

    def make_basis(u, _):
        make_angles(u)

        def rows(a8, _):
            some = pl.ds(pl.multiple_of(a8 * 8, 8), 8)
            for q in range(4):
                at = pl.ds(q * 128, 128)
                ua, va, cb, sb = UA[some, at], VA[some, at], CB[:, at], SB[:, at]
                for k in range(8):
                    value = ua[k:k + 1] * cb + va[k:k + 1] * sb
                    start = pl.multiple_of(a8 * 512, 512) + k * 64
                    basis[u, pl.ds(start, 64), at] = value.astype(BF16)
            return 0

        lax.fori_loop(0, HALF // 512, rows, 0)
        basis_copy(u).start()
        return 0

    lax.fori_loop(0, BEFORE, make_basis, 0)
    pl.semaphore_wait(barrier, 6 + WAVES - 1)

    BULKS = ((0, 1), (1, 1), (2, 2))

    def send(src, dst, to, send_sem, recv_sem):
        return pltpu.make_async_remote_copy(
            src_ref=src, dst_ref=dst, send_sem=send_sem, recv_sem=recv_sem,
            device_id=to, device_id_type=MESH,
        )

    def bytes_of(ref, send_sem, recv_sem):
        return send(ref, ref, step_first(0, 1), send_sem, recv_sem)

    def p1_start(kind, bulk):
        at, size = BULKS[bulk]
        ref = X.at[kind, pl.ds(at, size), second[kind], first[kind]]
        for by in (2, 1, 3):
            send(ref, ref, step_first(kind, by), p1_send.at[kind, bulk], p1_recv.at[kind, bulk]).start()

    def p1_all(kind, bulk):
        at, size = BULKS[bulk]
        ref = X.at[kind, pl.ds(at, size), second[kind], pl.ds(0, 3)]
        return bytes_of(ref, p1_send.at[kind, bulk], p1_recv.at[kind, bulk])

    def p2(kind, rho, which):
        d2 = second[kind]
        if which < 2:
            ref = X.at[kind, rho, d2]
        elif which == 2:
            ref = X.at[kind, rho, wrap(d2 - 1), :, 0]
        else:
            ref = X.at[kind, rho, wrap(d2 + 1), :, 1]
        to = step_second(kind, 1 if which % 2 == 0 else -1)
        return send(ref, ref, to, p2_send.at[kind, rho], p2_recv.at[kind, rho, min(which, 2)])

    def p2_direct(rho):
        for which in range(2):
            for kind in range(2):
                p2(kind, rho, which).start()

    def p2_row(kind, rho, which):
        ref = X.at[kind, rho, wrap(second[kind] + (-1 if which == 0 else 1))]
        bytes_of(ref, p2_send.at[kind, rho], p2_recv.at[kind, rho, which]).wait_recv()

    def p2_relayed(kind, rho):
        ref = X.at[kind, rho, wrap(second[kind] + 2)]
        bytes_of(ref, p2_send.at[kind, rho], p2_recv.at[kind, rho, 2]).wait_recv()

    def xe_start(stage):
        ref = XE.at[cy, cx] if stage == 0 else XE.at[cy]
        for by in (2, 1, 3):
            to = step_first(0, by) if stage == 0 else step_second(0, by)
            send(ref, ref, to, xe_send.at[stage], xe_recv.at[stage]).start()

    def xe_all(stage):
        ref = XE.at[cy, pl.ds(0, 3)] if stage == 0 else XE.at[pl.ds(0, 3)]
        return bytes_of(ref, xe_send.at[stage], xe_recv.at[stage])

    for bulk in range(3):
        for kind in range(2):
            p1_start(kind, bulk)
        if bulk == 0:
            xe_start(0)

    lax.fori_loop(BEFORE, BEFORE + 1, make_basis, 0)
    leg_copy.wait()

    def leg_pack(i, _):
        lo, swap = low_of(i)
        low = leg.at[2 * i + swap]
        high = leg.at[2 * i + 1 - swap]
        p = iota((64, 512), 1)
        rolled = pltpu.roll(high[:, 512:].astype(F32), lo, 1)
        LP[i, 0:64, 0:512] = jnp.where(p >= lo, low[:, 0:512].astype(F32), 0.0).astype(BF16)
        LP[i, 64:128, 0:512] = jnp.where(p < lo, rolled, 0.0).astype(BF16)
        LP[i, 0:64, 512:1024] = low[:, 512:]
        LP[i, 64:128, 512:1024] = jnp.zeros((64, 512), BF16)
        LP[i, 0:64, 1024:1152] = jnp.zeros((64, 128), BF16)
        moved = pltpu.roll(rolled[:, 384:], i + 1, 1)
        LP[i, 64:128, 1024:1152] = jnp.where(iota((64, 128), 1) == i, moved, 0.0).astype(BF16)
        return 0

    for kind in range(2):
        p1_all(kind, 0).wait_recv()
    p2_direct(0)
    xe_all(0).wait_recv()
    xe_start(1)
    lax.fori_loop(0, 4, leg_pack, 0)
    for kind in range(2):
        p1_all(kind, 1).wait_recv()
    p2_direct(1)
    lax.fori_loop(4, 8, leg_pack, 0)
    for kind in range(2):
        p1_all(kind, 2).wait_recv()

    def solve(x, kind, n, count):
        modes = dot(AHL[kind], x)
        modes = modes[0:256] + modes[256:512]
        factor = 1.0 / (1.0 + HM[:, 0:count] * (n * (n + 1.0)))
        out = []
        for r in range(2):
            part = modes[r * 128:(r + 1) * 128] * factor
            hi = part.astype(BF16)
            lo = (part - hi.astype(F32)).astype(BF16)
            both = jnp.concatenate([hi, hi], axis=0)
            out.append((dot(SS[...], both) + dot(SS[:, 0:128], lo)).astype(BF16))
        return out

    def field(kind, rho):
        i = 2 * rho + kind
        lo, _ = low_of(i)
        for h in range(2):
            p = iota((1, 512), 1) + h * 512
            n = jnp.where(p >= lo, p, p + 1024 - lo).astype(F32)
            x = X[kind, rho, :, :, h].reshape(256, 512)
            out = solve(x, kind, n, 512)
            for r in range(2):
                C[r * 128:(r + 1) * 128, h * 512:(h + 1) * 512] = out[r]
        contract = (((1,), (1,)), ((), ()))
        total = lax.dot_general(LP[i, :, 0:1024], C[...], contract, preferred_element_type=F32)
        total += lax.dot_general(LP[i, :, 1024:1152], CE[...], contract, preferred_element_type=F32)
        for r in range(2):
            for side in range(2):
                G32[pl.ds(r * 4 + kind * 2 + side, 64, stride=8)] = (
                    total[side * 64:(side + 1) * 64, r * 128:(r + 1) * 128]
                )

    def z_start(rho):
        G[rho] = G32[...].reshape(WAVES, 2, 16, 128).astype(BF16)

        def one(k, _):
            d = 8 + (1 - 2 * lax.rem(k, 2)) * (k // 2)
            to = lax.rem(w + d, WAVES)
            send(G.at[rho, to], F.at[rho, w], (to, col), z_send.at[rho], z_recv.at[rho]).start()
            return 0

        lax.fori_loop(1, WAVES, one, 0)
        F[rho, w] = G[rho, w]

    def z_all(rho):
        return bytes_of(F.at[rho, pl.ds(0, WAVES - 1)], z_send.at[rho], z_recv.at[rho])

    def values_copy(rho):
        return pltpu.make_async_copy(V.at[rho], values_hbm.at[rho], values_sem.at[rho])

    def make_values(rho):
        z_all(rho).wait_recv()
        sign = SG[rho * 128:(rho + 1) * 128]
        for u in range(4):
            tiles = F[rho, :, u // 2].astype(F32)
            at = (u % 2) * 8
            part = tiles[:, at:at + 8].reshape(128, 128)
            V[rho, u, :, 0:128] = part.astype(BF16)
            V[rho, u, :, 128:256] = (part * sign).astype(BF16)
        values_copy(rho).start()

    def relay(rho):
        for kind in range(2):
            for which in range(2):
                p2_row(kind, rho, which)
                p2(kind, rho, 2 + which).start()
        if rho < 2:
            p2_direct(rho + 2)

    relay(0)
    lax.fori_loop(BEFORE + 1, 4, make_basis, 0)
    xe_all(1).wait_recv()
    n = jnp.zeros((1, 128), F32)
    for i in range(8):
        lo, _ = low_of(i)
        n = jnp.where(iota((1, 128), 1) == i, (1023 - lo).astype(F32), n)
    out = solve(XE[...].reshape(256, 128), 0, n, 128)
    for r in range(2):
        CE[r * 128:(r + 1) * 128] = out[r]
    for rho in range(ROUNDS):
        if rho < 3:
            relay(rho + 1)
        if rho == 3:
            make_values(0)
        for kind in range(2):
            p2_relayed(kind, rho)
            field(kind, rho)
        z_start(rho)

    for kind in range(2):
        for bulk in range(3):
            p1_all(kind, bulk).wait_send()
        for rho in range(ROUNDS):
            ref = X.at[kind, rho, pl.ds(0, 3)]
            bytes_of(ref, p2_send.at[kind, rho], p2_recv.at[kind, rho, 0]).wait_send()
    for stage in range(2):
        xe_all(stage).wait_send()
    for u in range(4):
        basis_copy(u).wait()
    for rho in range(1, ROUNDS):
        make_values(rho)
    for rho in range(ROUNDS):
        z_all(rho).wait_send()
        values_copy(rho).wait()


def grid_kernel(cp_s, basis_hbm, values_hbm, out_hbm, basis, V, D, PL, stage, basis_sem, values_sem, out_sem):
    first = lax.axis_index("col") * 64 + lax.axis_index("wave") * 4

    def basis_copy(u, b):
        at = pl.ds(b * 1024, 1024)
        return pltpu.make_async_copy(basis_hbm.at[u, at], basis.at[u, at], basis_sem.at[u, b])

    def values_copy(u):
        return pltpu.make_async_copy(values_hbm.at[:, u], V.at[u], values_sem.at[u])

    def out_copy(u, b):
        at = pl.ds(b * 1024, 1024)
        return pltpu.make_async_copy(stage.at[u, at], out_hbm.at[0, u, at], out_sem.at[u, b])

    def fetch(u):
        values_copy(u).start()
        for b in range(2):
            basis_copy(u, b).start()

    def sums(u):
        values = V[u].reshape(512, 256)
        k = u % 2
        for b in range(2):
            both = dot(basis[u, b * 1024:(b + 1) * 1024], values)
            D[k, 1024 + b * 1024:2048 + b * 1024] = both[:, 128:256]
            if b == 0:
                stage[u, 0:1024] = both[:, 0:128].astype(BF16)
            else:
                PL[k, 1024:2048] = both[:, 0:128]

    def place(u):
        points = cp_s[first + u]
        half = points >> 1
        k = u % 2
        def turned(at):
            return D[k, pl.ds(pl.multiple_of(1024 + at - half, 8), 256)]
        for q in range(4, 16):
            at = q * 256
            j = iota((256, 128), 0) + at
            if q < 8:
                value = jnp.where(j < half, PL[k, at:at + 256], turned(at))
            else:
                value = jnp.where(j < points, turned(at), 0.0)
            stage[u, at:at + 256] = value.astype(BF16)

    for u in range(2):
        fetch(u)
    for u in range(5):
        if u < 4:
            values_copy(u).wait()
            basis_copy(u, 0).wait()
            basis_copy(u, 1).wait()
            if u < 2:
                fetch(u + 2)
            sums(u)
        if u > 0:
            place(u - 1)
        if u < 4:
            out_copy(u, 0).start()
        if u > 0:
            for b in range(1, 4):
                out_copy(u - 1, b).start()
    for u in range(4):
        for b in range(4):
            out_copy(u, b).wait()


def on_device(divergence, analysis, synthesis, helmholtz, legendre, wavenumbers, cycle_points):
    vmem = pl.BlockSpec(memory_space=pltpu.VMEM)
    smem = pl.BlockSpec(memory_space=pltpu.SMEM)
    hbm = pl.BlockSpec(memory_space=pl.ANY)
    dma = pltpu.SemaphoreType.DMA
    basis, values = pl.pallas_call(
        gather_kernel,
        out_shape=(
            jax.ShapeDtypeStruct((4, HALF, 512), BF16),
            jax.ShapeDtypeStruct((ROUNDS, 4, 128, 256), BF16),
        ),
        in_specs=[smem, smem, vmem, vmem, vmem, vmem, vmem, hbm],
        out_specs=(hbm, hbm),
        scratch_shapes=[
            pltpu.VMEM((2, ROUNDS, SIDE, SIDE, 2, 16, 512), BF16),
            pltpu.VMEM((SIDE, SIDE, 16, 128), BF16),
            pltpu.VMEM((16, 64, 1024), BF16),
            pltpu.VMEM((8, 128, 1152), BF16),
            pltpu.VMEM((2, 512, 256), BF16),
            pltpu.VMEM((128, 256), BF16),
            pltpu.VMEM((128, 512), F32),
            pltpu.VMEM((256, 1024), BF16),
            pltpu.VMEM((256, 128), BF16),
            pltpu.VMEM((512, 128), F32),
            pltpu.VMEM((ROUNDS, WAVES, 2, 16, 128), BF16),
            pltpu.VMEM((ROUNDS, WAVES, 2, 16, 128), BF16),
            pltpu.VMEM((8, 512), F32),
            pltpu.VMEM((512, 128), F32),
            pltpu.VMEM((32, 512), F32),
            pltpu.VMEM((32, 512), F32),
            pltpu.VMEM((64, 512), F32),
            pltpu.VMEM((64, 512), F32),
            pltpu.VMEM((4, HALF, 512), BF16),
            pltpu.VMEM((ROUNDS, 4, 128, 256), BF16),
            dma((2, 3)), dma((2, 3)),
            dma((2, ROUNDS)), dma((2, ROUNDS, 3)),
            dma((2,)), dma((2,)),
            dma((ROUNDS,)), dma((ROUNDS,)),
            dma(()), dma((4,)), dma((ROUNDS,)),
        ],
        compiler_params=pltpu.CompilerParams(
            collective_id=0, has_side_effects=True, vmem_limit_bytes=60 * MIB
        ),
        cost_estimate=pl.CostEstimate(flops=4 << 30, bytes_accessed=12 * MIB, transcendentals=0),
    )(
        wavenumbers, cycle_points, wavenumbers.reshape(1, 256), divergence, analysis, synthesis,
        helmholtz.reshape(1, 128), jnp.swapaxes(legendre, 1, 2),
    )
    return pl.pallas_call(
        grid_kernel,
        out_shape=jax.ShapeDtypeStruct((1, 4, LON, 128), BF16),
        in_specs=[smem, hbm, hbm],
        out_specs=hbm,
        scratch_shapes=[
            pltpu.VMEM((4, HALF, 512), BF16),
            pltpu.VMEM((4, ROUNDS, 128, 256), BF16),
            pltpu.VMEM((2, LON, 128), F32),
            pltpu.VMEM((2, HALF, 128), F32),
            pltpu.VMEM((4, LON, 128), BF16),
            dma((4, 2)), dma((4,)), dma((4, 4)),
        ],
        compiler_params=pltpu.CompilerParams(vmem_limit_bytes=60 * MIB),
        cost_estimate=pl.CostEstimate(flops=4 << 30, bytes_accessed=13 * MIB, transcendentals=0),
    )(cycle_points, basis, values)


def solution(mesh):
    placed = (P("wave", None, "col", None), P(), P(), P(), P("wave", None, "col"), P(), P())
    return jax.shard_map(
        on_device,
        mesh=mesh,
        in_specs=placed,
        out_specs=P("col", "wave", None, None),
        check_vma=False,
    )
```

```python
import math

import jax
import jax.numpy as jnp
from jax import lax
from jax.experimental import pallas as pl
from jax.experimental.pallas import tpu as pltpu
from jax.sharding import PartitionSpec as P

MESH = pl.DeviceIdType.MESH
F32 = jnp.float32
BF16 = jnp.bfloat16
LON = 4096
WAVES = 16
HALF = LON // 2
SIDE = 4
ROUNDS = 2
PAIRS = 8
BEFORE = 2
MIB = 1 << 20


def iota(shape, dim):
    return lax.broadcasted_iota(jnp.int32, shape, dim)


def dot(a, b):
    return jnp.dot(a, b, preferred_element_type=F32)


def cos_sin(turn):
    quadrant = jnp.floor(turn + 0.5)
    x = (turn - quadrant) * (0.5 * math.pi)
    z = x * x
    s = x * (1.0 + z * (-1.0 / 6 + z * (1.0 / 120 + z * (-1.0 / 5040 + z * (1.0 / 362880)))))
    c = 1.0 + z * (-0.5 + z * (1.0 / 24 + z * (-1.0 / 720 + z * (1.0 / 40320))))
    odd = (quadrant == 1.0) | (quadrant == 3.0)
    cosine = jnp.where(odd, s, c)
    sine = jnp.where(odd, c, s)
    cosine = jnp.where((quadrant == 1.0) | (quadrant == 2.0), -cosine, cosine)
    sine = jnp.where((quadrant == 2.0) | (quadrant == 3.0), -sine, sine)
    return cosine, sine


def gather_kernel(
    wn_s, cp_s, wn_v, div, analysis, synthesis, helm, leg_hbm, basis, V,
    X, N, XE, leg, OL, LN, RL, LP, AHL, SS, HM, C, CE, G32, G, F, ML, SG, UA, VA, CB, SB,
    p1_send, p1_recv, p2_send, p2_recv, xe_send, xe_recv, ln_send, ln_recv, z_send, z_recv,
    leg_sem,
):
    w = lax.axis_index("wave")
    col = lax.axis_index("col")
    cx, cy = col // SIDE, col % SIDE

    def wrap(v, n=SIDE):
        return lax.rem(v + n, n)

    first = (cx, cy)
    second = (cy, cx)

    def toward(d):
        by = 1 - 2 * (d % 2)
        return by, -by

    def held(kind, rho):
        return kind * 4 + 2 * rho + ((first[kind] + 1) // 2) % 2

    def given(kind, rho):
        return kind * 4 + 2 * rho + 1 - ((first[kind] + 1) // 2) % 2

    def column(kind, d1, d2):
        return d1 * SIDE + d2 if kind == 0 else d2 * SIDE + d1

    def step_first(kind, by):
        return (w, column(kind, wrap(first[kind] + by), second[kind]))

    def step_second(kind, by):
        return (w, column(kind, first[kind], wrap(second[kind] + by)))

    barrier = pltpu.get_barrier_semaphore()
    for kind in range(2):
        for by in (1, 2, 3):
            pl.semaphore_signal(barrier, inc=1, device_id=step_first(kind, by), device_id_type=MESH)

    partner_col = [step_first(kind, toward(first[kind])[0])[1] for kind in range(2)]

    def greet(d, _):
        for to in (col, partner_col[0], partner_col[1]):
            pl.semaphore_signal(
                barrier, inc=1, device_id=(lax.rem(w + d, WAVES), to), device_id_type=MESH
            )
        return 0

    lax.fori_loop(1, WAVES, greet, 0)
    leg_copy = pltpu.make_async_copy(leg_hbm, leg, leg_sem)
    leg_copy.start()

    def low_of(i):
        m = wn_s[w * 16 + 2 * i]
        return jnp.minimum(m, 1023 - m), jnp.where(m > 511, 1, 0)

    lanes = iota((16, 512), 1)
    tile_lane = iota((16, 128), 1)
    extra = jnp.zeros((16, 128), F32)
    for kind in range(2):
        for rho in range(ROUNDS):
            for keep in range(2):
                i = held(kind, rho) if keep else given(kind, rho)
                lo, swap = low_of(i)
                low = div[2 * i + swap].reshape(16, 1024)
                high = div[2 * i + 1 - swap].reshape(16, 1024)
                rolled = pltpu.roll(high[:, 512:], lo, 1)
                own = X.at[kind, rho, second[kind], first[kind]] if keep else N.at[kind, rho]
                own[0] = jnp.where(lanes >= lo, low[:, :512], rolled).astype(BF16)
                own[1] = low[:, 512:].astype(BF16)
                moved = pltpu.roll(rolled[:, 384:], i + 1, 1)
                extra = jnp.where(tile_lane == i, moved, extra)
    XE[cy, cx] = extra.astype(BF16)

    a_full = analysis[...]
    a_hi = a_full.astype(BF16)
    a_lo = (a_full - a_hi.astype(F32)).astype(BF16)
    row = iota((128, 256), 0)
    j = iota((128, 256), 1)
    j2, j1 = j >> 6, (j >> 4) & 3
    for kind in range(2):
        level = (j1 * SIDE + j2 if kind == 0 else j2 * SIDE + j1) * 8 + (j & 7)
        for r in range(2):
            pick = jnp.where((row == level) & (((j >> 3) & 1) == r), 1.0, 0.0).astype(BF16)
            AHL[kind, r * 128:(r + 1) * 128] = dot(a_hi, pick).astype(BF16)
            AHL[kind, 256 + r * 128:256 + (r + 1) * 128] = dot(a_lo, pick).astype(BF16)
    s_full = synthesis[...]
    s_hi = s_full.astype(BF16)
    SS[:, 0:128] = s_hi
    SS[:, 128:256] = (s_full - s_hi.astype(F32)).astype(BF16)
    h_rows = jnp.broadcast_to(helm[...], (128, 128)).T
    for q in range(4):
        HM[:, q * 128:(q + 1) * 128] = h_rows

    lane = iota((256, 512), 1)
    slot = ((lane >> 2) & 15) * 16 + 2 * (lane >> 6)
    choose = jnp.where(iota((256, 512), 0) == slot, 1.0, 0.0).astype(BF16)
    wn = jnp.broadcast_to(wn_v[...], (16, 256))
    upper = dot((wn >> 5).astype(F32).astype(BF16), choose)
    lower = dot((wn & 31).astype(F32).astype(BF16), choose)
    m0 = (upper * 32.0 + lower)[0:8]
    m_lo = jnp.minimum(m0, 1023.0 - m0)
    m_lane = jnp.where((iota((8, 512), 1) & 1) == 1, 1023.0 - m_lo, m_lo)
    ML[...] = m_lane
    sign = 1.0 - 2.0 * (m_lane - 2.0 * jnp.floor(m_lane * 0.5))
    for q in range(4):
        part = jnp.broadcast_to(sign[0:1, q * 128:(q + 1) * 128], (128, 128))
        SG[q * 128:(q + 1) * 128] = part.T

    def make_angles(u):
        latitude = col * 64 + w * 4 + u

        def angle(index, count):
            points = jnp.full((count, 512), cp_s[latitude], jnp.int32).astype(F32)
            inverse = 1.0 / points
            product = index.astype(F32) * jnp.broadcast_to(ML[0:1], (count, 512))
            rest = product - jnp.floor(product * inverse) * points
            rest = jnp.where(rest < 0.0, rest + points, rest)
            rest = jnp.where(rest >= points, rest - points, rest)
            return cos_sin(rest * (4.0 * inverse))

        c, s = angle(iota((32, 512), 0) * 64, 32)
        weight = jnp.where(ML[0:1] == 0.0, 1.0, 2.0) / math.sqrt(256.0)
        imaginary = ((iota((32, 512), 1) >> 1) & 1) == 1
        c, s = weight * c, -weight * s
        UA[...] = jnp.where(imaginary, s, c)
        VA[...] = jnp.where(imaginary, -c, s)
        c, s = angle(iota((64, 512), 0), 64)
        CB[...] = c
        SB[...] = s

    def make_basis(u, _):
        make_angles(u)

        def rows(a8, _):
            some = pl.ds(pl.multiple_of(a8 * 8, 8), 8)
            for q in range(4):
                at = pl.ds(q * 128, 128)
                ua, va, cb, sb = UA[some, at], VA[some, at], CB[:, at], SB[:, at]
                for k in range(8):
                    value = ua[k:k + 1] * cb + va[k:k + 1] * sb
                    start = pl.multiple_of(a8 * 512, 512) + k * 64
                    basis[u, pl.ds(start, 64), at] = value.astype(BF16)
            return 0

        lax.fori_loop(0, HALF // 512, rows, 0)
        return 0

    def leg_pack(i, to):
        lo, swap = low_of(i)
        low = leg.at[2 * i + swap]
        high = leg.at[2 * i + 1 - swap]
        rolled = pltpu.roll(high[:, 512:].astype(F32), lo, 1)
        both = jnp.where(iota((64, 512), 1) >= lo, low[:, 0:512].astype(F32), rolled)
        to[:, 0:512] = both.astype(BF16)
        to[:, 512:1024] = low[:, 512:]
        moved = pltpu.roll(rolled[:, 384:], i + 1, 1)
        to[:, 1024:1152] = jnp.where(iota((64, 128), 1) == i, moved, 0.0).astype(BF16)

    def leg_spread(kind, rho, at, block):
        lo, _ = low_of(held(kind, rho))
        p = iota((64, 512), 1)
        both = block[:, 0:512].astype(F32)
        to = LP.at[kind, rho]
        to[at:at + 64, 0:512] = jnp.where(p >= lo, both, 0.0).astype(BF16)
        to[at + 64:at + 128, 0:512] = jnp.where(p < lo, both, 0.0).astype(BF16)
        to[at:at + 64, 512:1024] = block[:, 512:1024]
        to[at + 64:at + 128, 512:1024] = jnp.zeros((64, 512), BF16)
        to[at:at + 64, 1024:1152] = jnp.zeros((64, 128), BF16)
        to[at + 64:at + 128, 1024:1152] = block[:, 1024:1152]

    leg_copy.wait()
    for rho in range(ROUNDS):
        for kind in range(2):
            leg_pack(given(kind, rho), LN.at[kind, rho])
    lax.fori_loop(0, BEFORE, make_basis, 0)
    pl.semaphore_wait(barrier, 6 + 3 * (WAVES - 1))

    def send(src, dst, to, send_sem, recv_sem):
        return pltpu.make_async_remote_copy(
            src_ref=src, dst_ref=dst, send_sem=send_sem, recv_sem=recv_sem,
            device_id=to, device_id_type=MESH,
        )

    def bytes_of(ref, send_sem, recv_sem):
        return send(ref, ref, step_first(0, 1), send_sem, recv_sem)

    def p1_start(kind, rho):
        to = X.at[kind, rho, second[kind], first[kind]]
        partner, other = toward(first[kind])
        for src, by in ((N.at[kind, rho], 2), (N.at[kind, rho], partner), (to, other)):
            send(src, to, step_first(kind, by), p1_send.at[kind, rho], p1_recv.at[kind, rho]).start()

    def p1_all(kind, rho):
        ref = X.at[kind, rho, second[kind], pl.ds(0, 3)]
        return bytes_of(ref, p1_send.at[kind, rho], p1_recv.at[kind, rho])

    def p2(kind, rho, which):
        d2 = second[kind]
        partner, other = toward(d2)
        ref = X.at[kind, rho, wrap(d2 + partner) if which == 2 else d2]
        to = step_second(kind, partner if which == 0 else other)
        return send(ref, ref, to, p2_send.at[kind, rho], p2_recv.at[kind, rho, which])

    def p2_direct(rho):
        for which in range(2):
            for kind in range(2):
                p2(kind, rho, which).start()

    def p2_arrived(kind, rho, which):
        partner, other = toward(second[kind])
        ref = X.at[kind, rho, wrap(second[kind] + (partner, other, 2)[which])]
        bytes_of(ref, p2_send.at[kind, rho], p2_recv.at[kind, rho, which]).wait_recv()

    def ln(kind, rho):
        to = step_first(kind, toward(first[kind])[0])
        return send(LN.at[kind, rho], RL.at[kind, rho], to, ln_send.at[kind, rho], ln_recv.at[kind, rho])

    def xe_start(stage):
        ref = XE.at[cy, cx] if stage == 0 else XE.at[cy]
        for by in (2, 1, 3):
            to = step_first(0, by) if stage == 0 else step_second(0, by)
            send(ref, ref, to, xe_send.at[stage], xe_recv.at[stage]).start()

    def xe_all(stage):
        ref = XE.at[cy, pl.ds(0, 3)] if stage == 0 else XE.at[pl.ds(0, 3)]
        return bytes_of(ref, xe_send.at[stage], xe_recv.at[stage])

    for rho in range(ROUNDS):
        for kind in range(2):
            p1_start(kind, rho)
        if rho == 0:
            xe_start(0)
    for kind in range(2):
        ln(kind, 0).start()

    for rho in range(ROUNDS):
        for kind in range(2):
            leg_pack(held(kind, rho), OL.at[kind, rho])
            leg_spread(kind, rho, 0, OL.at[kind, rho])
    lax.fori_loop(BEFORE, BEFORE + 1, make_basis, 0)
    for rho in range(ROUNDS):
        for kind in range(2):
            p1_all(kind, rho).wait_recv()
        p2_direct(rho)
    for kind in range(2):
        ln(kind, 1).start()
    xe_all(0).wait_recv()
    xe_start(1)
    lax.fori_loop(BEFORE + 1, 4, make_basis, 0)

    def solve(x, kind, n, count):
        modes = dot(AHL[kind], x)
        modes = modes[0:256] + modes[256:512]
        factor = 1.0 / (1.0 + HM[:, 0:count] * (n * (n + 1.0)))
        out = []
        for r in range(2):
            part = modes[r * 128:(r + 1) * 128] * factor
            hi = part.astype(BF16)
            lo = (part - hi.astype(F32)).astype(BF16)
            both = jnp.concatenate([hi, hi], axis=0)
            out.append((dot(SS[...], both) + dot(SS[:, 0:128], lo)).astype(BF16))
        return out

    def field(kind, rho):
        lo, _ = low_of(held(kind, rho))
        for h in range(2):
            p = iota((1, 512), 1) + h * 512
            n = jnp.where(p >= lo, p, p + 1024 - lo).astype(F32)
            x = X[kind, rho, :, :, h].reshape(256, 512)
            out = solve(x, kind, n, 512)
            for r in range(2):
                C[r * 128:(r + 1) * 128, h * 512:(h + 1) * 512] = out[r]
        table = LP.at[kind, rho]
        contract = (((1,), (1,)), ((), ()))
        total = lax.dot_general(table[:, 0:1024], C[...], contract, preferred_element_type=F32)
        total += lax.dot_general(table[:, 1024:1152], CE[...], contract, preferred_element_type=F32)
        for block in range(2):
            for side in range(2):
                for r in range(2):
                    at = block * 128 + side * 64
                    G32[block, pl.ds(r * 2 + side, 64, stride=4)] = (
                        total[at:at + 64, r * 128:(r + 1) * 128]
                    )

    def z_start(kind, rho):
        i = held(kind, rho)
        for block in range(2):
            G[kind, rho, block] = G32[block].reshape(WAVES, 16, 128).astype(BF16)

        def block_to(block, to):
            there = (to, partner_col[kind] if block else col)
            send(G.at[kind, rho, block, to], F.at[i, w], there, z_send.at[kind, rho, block],
                 z_recv.at[i]).start()

        def one(k, _):
            d = 8 + (1 - 2 * lax.rem(k, 2)) * (k // 2)
            to = lax.rem(w + d, WAVES)
            block_to(1, to)
            block_to(0, to)
            return 0

        lax.fori_loop(1, WAVES, one, 0)
        block_to(1, w)
        F[i, w] = G[kind, rho, 0, w]

    def z_sent(kind, rho):
        for block in range(2):
            ref = F.at[0, pl.ds(0, WAVES - 1 + block)]
            bytes_of(ref, z_send.at[kind, rho, block], z_recv.at[0]).wait_send()

    def make_values(kind, rho, mine):
        i = held(kind, rho) if mine else given(kind, rho)
        ref = F.at[i, pl.ds(0, WAVES - 1 if mine else WAVES)]
        bytes_of(ref, z_send.at[kind, rho, 0], z_recv.at[i]).wait_recv()
        sign = SG[pl.ds(pl.multiple_of(i * 64, 64), 64)]
        tiles = F[i].astype(F32).reshape(8, 2, 2, 8, 128)
        top = iota((64, 128), 0) % 8 < 4
        for u2 in range(2):
            even = tiles[:, 0, u2].reshape(64, 128)
            odd = tiles[:, 1, u2].reshape(64, 128)
            swap_even = pltpu.roll(tiles[:, 0, u2], 4, 1).reshape(64, 128)
            swap_odd = pltpu.roll(tiles[:, 1, u2], 4, 1).reshape(64, 128)
            for u1 in range(2):
                part = jnp.where(top, even, swap_odd) if u1 == 0 else jnp.where(top, swap_even, odd)
                V[i, 2 * u2 + u1, :, 0:128] = part.astype(BF16)
                V[i, 2 * u2 + u1, :, 128:256] = (part * sign).astype(BF16)

    def relay(rho):
        for kind in range(2):
            p2_arrived(kind, rho, 0)
            p2(kind, rho, 2).start()

    relay(0)
    xe_all(1).wait_recv()
    n = jnp.zeros((1, 128), F32)
    for i in range(8):
        lo, _ = low_of(i)
        n = jnp.where(iota((1, 128), 1) == i, (1023 - lo).astype(F32), n)
    out = solve(XE[...].reshape(256, 128), 0, n, 128)
    for r in range(2):
        CE[r * 128:(r + 1) * 128] = out[r]
    relay(1)
    for rho in range(ROUNDS):
        for kind in range(2):
            p2_arrived(kind, rho, 1)
            ln(kind, rho).wait_recv()
            leg_spread(kind, rho, 128, RL.at[kind, rho])
            p2_arrived(kind, rho, 2)
            field(kind, rho)
            z_start(kind, rho)

    for kind in range(2):
        for rho in range(ROUNDS):
            make_values(kind, rho, True)
            make_values(kind, rho, False)
            if rho == 0 and kind == 0:
                for k in range(2):
                    for r in range(ROUNDS):
                        p1_all(k, r).wait_send()
                        ln(k, r).wait_send()
                        ref = X.at[k, r, pl.ds(0, 3)]
                        bytes_of(ref, p2_send.at[k, r], p2_recv.at[k, r, 0]).wait_send()
                for stage in range(2):
                    xe_all(stage).wait_send()
    for kind in range(2):
        for rho in range(ROUNDS):
            z_sent(kind, rho)


def grid_kernel(cp_s, basis, V, out_hbm, D, PL, stage, out_sem):
    first = lax.axis_index("col") * 64 + lax.axis_index("wave") * 4

    def out_copy(u, b):
        at = pl.ds(b * 1024, 1024)
        return pltpu.make_async_copy(stage.at[u, at], out_hbm.at[0, u, at], out_sem.at[u, b])

    def sums(u):
        values = V[:, u].reshape(512, 256)
        k = u % 2
        for b in range(2):
            both = dot(basis[u, b * 1024:(b + 1) * 1024], values)
            D[k, 1024 + b * 1024:2048 + b * 1024] = both[:, 128:256]
            if b == 0:
                stage[u, 0:1024] = both[:, 0:128].astype(BF16)
            else:
                PL[k, 1024:2048] = both[:, 0:128]

    def place(u):
        points = cp_s[first + u]
        half = points >> 1
        k = u % 2
        def turned(at):
            return D[k, pl.ds(pl.multiple_of(1024 + at - half, 8), 256)]
        for q in range(4, 16):
            at = q * 256
            j = iota((256, 128), 0) + at
            if q < 8:
                value = jnp.where(j < half, PL[k, at:at + 256], turned(at))
            else:
                value = jnp.where(j < points, turned(at), 0.0)
            stage[u, at:at + 256] = value.astype(BF16)

    for u in range(5):
        if u < 4:
            sums(u)
        if u > 0:
            place(u - 1)
        if u < 4:
            out_copy(u, 0).start()
        if u > 0:
            for b in range(1, 4):
                out_copy(u - 1, b).start()
    for u in range(4):
        for b in range(4):
            out_copy(u, b).wait()


def on_device(divergence, analysis, synthesis, helmholtz, legendre, wavenumbers, cycle_points):
    vmem = pl.BlockSpec(memory_space=pltpu.VMEM)
    smem = pl.BlockSpec(memory_space=pltpu.SMEM)
    hbm = pl.BlockSpec(memory_space=pl.ANY)
    dma = pltpu.SemaphoreType.DMA
    basis, values = pl.pallas_call(
        gather_kernel,
        out_shape=(
            pltpu.VMEM((4, HALF, 512), BF16),
            pltpu.VMEM((PAIRS, 4, 64, 256), BF16),
        ),
        in_specs=[smem, smem, vmem, vmem, vmem, vmem, vmem, hbm],
        out_specs=(vmem, vmem),
        scratch_shapes=[
            pltpu.VMEM((2, ROUNDS, SIDE, SIDE, 2, 16, 512), BF16),
            pltpu.VMEM((2, ROUNDS, 2, 16, 512), BF16),
            pltpu.VMEM((SIDE, SIDE, 16, 128), BF16),
            pltpu.VMEM((16, 64, 1024), BF16),
            pltpu.VMEM((2, ROUNDS, 64, 1152), BF16),
            pltpu.VMEM((2, ROUNDS, 64, 1152), BF16),
            pltpu.VMEM((2, ROUNDS, 64, 1152), BF16),
            pltpu.VMEM((2, ROUNDS, 256, 1152), BF16),
            pltpu.VMEM((2, 512, 256), BF16),
            pltpu.VMEM((128, 256), BF16),
            pltpu.VMEM((128, 512), F32),
            pltpu.VMEM((256, 1024), BF16),
            pltpu.VMEM((256, 128), BF16),
            pltpu.VMEM((2, 256, 128), F32),
            pltpu.VMEM((2, ROUNDS, 2, WAVES, 16, 128), BF16),
            pltpu.VMEM((PAIRS, WAVES, 16, 128), BF16),
            pltpu.VMEM((8, 512), F32),
            pltpu.VMEM((512, 128), F32),
            pltpu.VMEM((32, 512), F32),
            pltpu.VMEM((32, 512), F32),
            pltpu.VMEM((64, 512), F32),
            pltpu.VMEM((64, 512), F32),
            dma((2, ROUNDS)), dma((2, ROUNDS)),
            dma((2, ROUNDS)), dma((2, ROUNDS, 3)),
            dma((2,)), dma((2,)),
            dma((2, ROUNDS)), dma((2, ROUNDS)),
            dma((2, ROUNDS, 2)), dma((PAIRS,)),
            dma(()),
        ],
        compiler_params=pltpu.CompilerParams(
            collective_id=0, has_side_effects=True, vmem_limit_bytes=50 * MIB
        ),
        cost_estimate=pl.CostEstimate(flops=4 << 30, bytes_accessed=12 * MIB, transcendentals=0),
    )(
        wavenumbers, cycle_points, wavenumbers.reshape(1, 256), divergence, analysis, synthesis,
        helmholtz.reshape(1, 128), jnp.swapaxes(legendre, 1, 2),
    )
    return pl.pallas_call(
        grid_kernel,
        out_shape=jax.ShapeDtypeStruct((1, 4, LON, 128), BF16),
        in_specs=[smem, vmem, vmem],
        out_specs=hbm,
        scratch_shapes=[
            pltpu.VMEM((2, LON, 128), F32),
            pltpu.VMEM((2, HALF, 128), F32),
            pltpu.VMEM((4, LON, 128), BF16),
            dma((4, 4)),
        ],
        compiler_params=pltpu.CompilerParams(vmem_limit_bytes=30 * MIB),
        cost_estimate=pl.CostEstimate(flops=4 << 30, bytes_accessed=13 * MIB, transcendentals=0),
    )(cycle_points, basis, values)


def solution(mesh):
    placed = (P("wave", None, "col", None), P(), P(), P(), P("wave", None, "col"), P(), P())
    return jax.shard_map(
        on_device,
        mesh=mesh,
        in_specs=placed,
        out_specs=P("col", "wave", None, None),
        check_vma=False,
    )
```

```python
import math

import jax
import jax.numpy as jnp
from jax import lax
from jax.experimental import pallas as pl
from jax.experimental.pallas import tpu as pltpu
from jax.sharding import PartitionSpec as P

MESH = pl.DeviceIdType.MESH
F32 = jnp.float32
BF16 = jnp.bfloat16
LON = 4096
WAVES = 16
HALF = LON // 2
SIDE = 4
ROUNDS = 2
PAIRS = 8
FIRST, SECOND = 1, 2
MIB = 1 << 20


def iota(shape, dim):
    return lax.broadcasted_iota(jnp.int32, shape, dim)


def dot(a, b):
    return jnp.dot(a, b, preferred_element_type=F32)


def cos_sin(turn):
    quadrant = jnp.floor(turn + 0.5)
    x = (turn - quadrant) * (0.5 * math.pi)
    z = x * x
    s = x * (1.0 + z * (-1.0 / 6 + z * (1.0 / 120 + z * (-1.0 / 5040 + z * (1.0 / 362880)))))
    c = 1.0 + z * (-0.5 + z * (1.0 / 24 + z * (-1.0 / 720 + z * (1.0 / 40320))))
    odd = (quadrant == 1.0) | (quadrant == 3.0)
    cosine = jnp.where(odd, s, c)
    sine = jnp.where(odd, c, s)
    cosine = jnp.where((quadrant == 1.0) | (quadrant == 2.0), -cosine, cosine)
    sine = jnp.where((quadrant == 2.0) | (quadrant == 3.0), -sine, sine)
    return cosine, sine


def gather_kernel(
    wn_hbm, cp_hbm, wn_row, div_hbm, analysis_hbm, synthesis_hbm, helm_hbm, leg_hbm, basis, V,
    wn_s, cp_s, wn_v, div, analysis, synthesis, helm,
    X, N, XE, leg, OL, LN, RL, LP, AHL, SS, HM, C, G32, G, F, ML, SG, UA, VA, CB, SB,
    p1_send, p1_recv, p2_send, p2_recv, xe_send, xe_recv, ln_send, ln_recv, z_send, z_recv,
    leg_sem, in_sem,
):
    w = lax.axis_index("wave")
    col = lax.axis_index("col")
    cx, cy = col // SIDE, col % SIDE

    def wrap(v, n=SIDE):
        return lax.rem(v + n, n)

    first = (cx, cy)
    second = (cy, cx)

    def toward(d):
        by = 1 - 2 * (d % 2)
        return by, -by

    def held(kind, rho):
        return kind * 4 + 2 * rho + ((first[kind] + 1) // 2) % 2

    def given(kind, rho):
        return kind * 4 + 2 * rho + 1 - ((first[kind] + 1) // 2) % 2

    def column(kind, d1, d2):
        return d1 * SIDE + d2 if kind == 0 else d2 * SIDE + d1

    def step_first(kind, by):
        return (w, column(kind, wrap(first[kind] + by), second[kind]))

    def step_second(kind, by):
        return (w, column(kind, first[kind], wrap(second[kind] + by)))

    fetches = [
        pltpu.make_async_copy(src, dst, in_sem.at[k])
        for k, (src, dst) in enumerate((
            (wn_hbm, wn_s), (div_hbm, div), (cp_hbm, cp_s), (wn_row, wn_v),
            (analysis_hbm, analysis), (synthesis_hbm, synthesis), (helm_hbm, helm),
        ))
    ]
    for fetch in fetches:
        fetch.start()
    barrier = pltpu.get_barrier_semaphore()
    for kind in range(2):
        for by in (1, 2, 3):
            pl.semaphore_signal(barrier, inc=1, device_id=step_first(kind, by), device_id_type=MESH)

    partner_col = [step_first(kind, toward(first[kind])[0])[1] for kind in range(2)]

    def greet(d, _):
        for to in (col, partner_col[0], partner_col[1]):
            pl.semaphore_signal(
                barrier, inc=1, device_id=(lax.rem(w + d, WAVES), to), device_id_type=MESH
            )
        return 0

    lax.fori_loop(1, WAVES, greet, 0)
    leg_copy = pltpu.make_async_copy(leg_hbm, leg, leg_sem)
    leg_copy.start()

    def low_of(i):
        m = wn_s[w * 16 + 2 * i]
        return jnp.minimum(m, 1023 - m), jnp.where(m > 511, 1, 0)

    for fetch in fetches:
        fetch.wait()

    lanes = iota((16, 512), 1)
    tile_lane = iota((16, 128), 1)
    extra = jnp.zeros((16, 128), F32)
    for kind in range(2):
        for rho in range(ROUNDS):
            for keep in range(2):
                i = held(kind, rho) if keep else given(kind, rho)
                lo, swap = low_of(i)
                low = div[2 * i + swap].reshape(16, 1024)
                high = div[2 * i + 1 - swap].reshape(16, 1024)
                rolled = pltpu.roll(high[:, 512:], lo, 1)
                own = X.at[kind, rho, second[kind], 0] if keep else N.at[kind, rho]
                own[0] = jnp.where(lanes >= lo, low[:, :512], rolled).astype(BF16)
                own[1] = low[:, 512:].astype(BF16)
                moved = pltpu.roll(rolled[:, 384:], i + 1, 1)
                extra = jnp.where(tile_lane == i, moved, extra)
    XE[cy, 0] = extra.astype(BF16)

    def make_angles(u):
        latitude = col * 64 + w * 4 + u

        def angle(index, count):
            points = jnp.full((count, 512), cp_s[latitude], jnp.int32).astype(F32)
            inverse = 1.0 / points
            product = index.astype(F32) * jnp.broadcast_to(ML[0:1], (count, 512))
            rest = product - jnp.floor(product * inverse) * points
            rest = jnp.where(rest < 0.0, rest + points, rest)
            rest = jnp.where(rest >= points, rest - points, rest)
            return cos_sin(rest * (4.0 * inverse))

        c, s = angle(iota((32, 512), 0) * 64, 32)
        weight = jnp.where(ML[0:1] == 0.0, 1.0, 2.0) / math.sqrt(256.0)
        imaginary = ((iota((32, 512), 1) >> 1) & 1) == 1
        c, s = weight * c, -weight * s
        UA[...] = jnp.where(imaginary, s, c)
        VA[...] = jnp.where(imaginary, -c, s)
        c, s = angle(iota((64, 512), 0), 64)
        CB[...] = c
        SB[...] = s

    def make_basis(u, _):
        make_angles(u)

        def rows(a8, _):
            some = pl.ds(pl.multiple_of(a8 * 8, 8), 8)
            for q in range(4):
                at = pl.ds(q * 128, 128)
                ua, va, cb, sb = UA[some, at], VA[some, at], CB[:, at], SB[:, at]
                for k in range(8):
                    value = ua[k:k + 1] * cb + va[k:k + 1] * sb
                    start = pl.multiple_of(a8 * 512, 512) + k * 64
                    basis[u, pl.ds(start, 64), at] = value.astype(BF16)
            return 0

        lax.fori_loop(0, HALF // 512, rows, 0)
        return 0

    def leg_pack(i, to):
        lo, swap = low_of(i)
        low = leg.at[2 * i + swap]
        high = leg.at[2 * i + 1 - swap]
        rolled = pltpu.roll(high[:, 512:].astype(F32), lo, 1)
        both = jnp.where(iota((64, 512), 1) >= lo, low[:, 0:512].astype(F32), rolled)
        to[:, 0:512] = both.astype(BF16)
        to[:, 512:1024] = low[:, 512:]
        moved = pltpu.roll(rolled[:, 384:], i + 1, 1)
        to[:, 1024:1152] = jnp.where(iota((64, 128), 1) == i, moved, 0.0).astype(BF16)

    def leg_spread(kind, rho, at, block):
        lo, _ = low_of(held(kind, rho))
        p = iota((64, 512), 1)
        both = block[:, 0:512].astype(F32)
        to = LP.at[kind, rho]
        to[at:at + 64, 0:512] = jnp.where(p >= lo, both, 0.0).astype(BF16)
        to[at + 64:at + 128, 0:512] = jnp.where(p < lo, both, 0.0).astype(BF16)
        to[at:at + 64, 512:1024] = block[:, 512:1024]
        to[at + 64:at + 128, 512:1024] = jnp.zeros((64, 512), BF16)
        to[at:at + 64, 1024:1152] = jnp.zeros((64, 128), BF16)
        to[at + 64:at + 128, 1024:1152] = block[:, 1024:1152]

    pl.semaphore_wait(barrier, 6 + 3 * (WAVES - 1))

    def send(src, dst, to, send_sem, recv_sem):
        return pltpu.make_async_remote_copy(
            src_ref=src, dst_ref=dst, send_sem=send_sem, recv_sem=recv_sem,
            device_id=to, device_id_type=MESH,
        )

    def bytes_of(ref, send_sem, recv_sem):
        return send(ref, ref, step_first(0, 1), send_sem, recv_sem)

    def p1_start(kind, rho):
        own = X.at[kind, rho, second[kind], 0]
        partner, other = toward(first[kind])
        for src, by in ((N.at[kind, rho], 2), (N.at[kind, rho], partner), (own, other)):
            to = X.at[kind, rho, second[kind], wrap(-by)]
            send(src, to, step_first(kind, by), p1_send.at[kind, rho], p1_recv.at[kind, rho]).start()

    def p1_all(kind, rho):
        ref = X.at[kind, rho, second[kind], pl.ds(0, 3)]
        return bytes_of(ref, p1_send.at[kind, rho], p1_recv.at[kind, rho])

    def p2(kind, rho, part, which):
        d2 = second[kind]
        partner, other = toward(d2)
        row = wrap(d2 + partner) if which == 2 else d2
        ref = X.at[kind, rho, row, pl.ds(0, 1) if part == 0 else pl.ds(1, 3)]
        to = step_second(kind, partner if which == 0 else other)
        return send(ref, ref, to, p2_send.at[kind, rho], p2_recv.at[kind, rho, part, which])

    def p2_direct(rho, part):
        for which in range(2):
            for kind in range(2):
                p2(kind, rho, part, which).start()

    def p2_arrived(kind, rho, part, which):
        partner, other = toward(second[kind])
        row = wrap(second[kind] + (partner, other, 2)[which])
        ref = X.at[kind, rho, row, pl.ds(0, 1) if part == 0 else pl.ds(1, 3)]
        bytes_of(ref, p2_send.at[kind, rho], p2_recv.at[kind, rho, part, which]).wait_recv()

    def ln(kind, rho):
        to = step_first(kind, toward(first[kind])[0])
        return send(LN.at[kind, rho], RL.at[kind, rho], to, ln_send.at[kind, rho], ln_recv.at[kind, rho])

    def relay(rho, part):
        for kind in range(2):
            p2_arrived(kind, rho, part, 0)
            p2(kind, rho, part, 2).start()

    def xe_start(stage):
        for by in (2, 1, 3):
            src = XE.at[cy, 0] if stage == 0 else XE.at[cy]
            dst = XE.at[cy, 4 - by] if stage == 0 else XE.at[cy]
            to = step_first(0, by) if stage == 0 else step_second(0, by)
            send(src, dst, to, xe_send.at[stage], xe_recv.at[stage]).start()

    def xe_all(stage):
        ref = XE.at[cy, pl.ds(0, 3)] if stage == 0 else XE.at[pl.ds(0, 3)]
        return bytes_of(ref, xe_send.at[stage], xe_recv.at[stage])

    for rho in range(ROUNDS):
        for kind in range(2):
            p1_start(kind, rho)
        if rho == 0:
            xe_start(0)
    for rho in range(ROUNDS):
        p2_direct(rho, 0)

    a_full = analysis[...]
    a_hi = a_full.astype(BF16)
    a_lo = (a_full - a_hi.astype(F32)).astype(BF16)
    row = iota((128, 256), 0)
    j = iota((128, 256), 1)
    j2, j1 = j >> 6, (j >> 4) & 3
    for kind in range(2):
        j_first = (j1 + first[kind]) & 3
        level = column(kind, j_first, j2) * 8 + (j & 7)
        for r in range(2):
            pick = jnp.where((row == level) & (((j >> 3) & 1) == r), 1.0, 0.0).astype(BF16)
            AHL[kind, r * 128:(r + 1) * 128] = dot(a_hi, pick).astype(BF16)
            AHL[kind, 256 + r * 128:256 + (r + 1) * 128] = dot(a_lo, pick).astype(BF16)
    s_full = synthesis[...]
    s_hi = s_full.astype(BF16)
    SS[:, 0:128] = s_hi
    SS[:, 128:256] = (s_full - s_hi.astype(F32)).astype(BF16)
    h_rows = jnp.broadcast_to(helm[...], (128, 128)).T
    for q in range(4):
        HM[:, q * 128:(q + 1) * 128] = h_rows

    lane = iota((256, 512), 1)
    slot = ((lane >> 2) & 15) * 16 + 2 * (lane >> 6)
    choose = jnp.where(iota((256, 512), 0) == slot, 1.0, 0.0).astype(BF16)
    wn = jnp.broadcast_to(wn_v[...], (16, 256))
    upper = dot((wn >> 5).astype(F32).astype(BF16), choose)
    lower = dot((wn & 31).astype(F32).astype(BF16), choose)
    m0 = (upper * 32.0 + lower)[0:8]
    m_lo = jnp.minimum(m0, 1023.0 - m0)
    m_lane = jnp.where((iota((8, 512), 1) & 1) == 1, 1023.0 - m_lo, m_lo)
    ML[...] = m_lane
    sign = 1.0 - 2.0 * (m_lane - 2.0 * jnp.floor(m_lane * 0.5))
    for q in range(4):
        part = jnp.broadcast_to(sign[0:1, q * 128:(q + 1) * 128], (128, 128))
        SG[q * 128:(q + 1) * 128] = part.T

    leg_copy.wait()
    for rho in range(ROUNDS):
        for kind in range(2):
            leg_pack(given(kind, rho), LN.at[kind, rho])
    for rho in range(ROUNDS):
        for kind in range(2):
            p1_all(kind, rho).wait_recv()
        if rho == 0:
            xe_all(0).wait_recv()
            xe_start(1)
        p2_direct(rho, 1)
    for rho in range(ROUNDS):
        relay(rho, 0)
    for kind in range(2):
        ln(kind, 0).start()
    for rho in range(ROUNDS):
        for kind in range(2):
            leg_pack(held(kind, rho), OL.at[kind, rho])
            leg_spread(kind, rho, 0, OL.at[kind, rho])
    lax.fori_loop(0, FIRST, make_basis, 0)

    def solve(x, kind, n, count):
        modes = dot(AHL[kind], x)
        modes = modes[0:256] + modes[256:512]
        factor = 1.0 / (1.0 + HM[:, 0:count] * (n * (n + 1.0)))
        out = []
        for r in range(2):
            part = modes[r * 128:(r + 1) * 128] * factor
            hi = part.astype(BF16)
            lo = (part - hi.astype(F32)).astype(BF16)
            both = jnp.concatenate([hi, hi], axis=0)
            out.append((dot(SS[...], both) + dot(SS[:, 0:128], lo)).astype(BF16))
        return out

    def field(kind, rho):
        lo, _ = low_of(held(kind, rho))
        for h in range(2):
            p = iota((1, 512), 1) + h * 512
            n = jnp.where(p >= lo, p, p + 1024 - lo).astype(F32)
            x = X[kind, rho, :, :, h].reshape(256, 512)
            out = solve(x, kind, n, 512)
            for r in range(2):
                C[r * 128:(r + 1) * 128, h * 512:(h + 1) * 512] = out[r]
        table = LP.at[kind, rho]
        contract = (((1,), (1,)), ((), ()))
        total = lax.dot_general(table[...], C[...], contract, preferred_element_type=F32)
        for block in range(2):
            for side in range(2):
                for r in range(2):
                    at = block * 128 + side * 64
                    G32[block, pl.ds(r * 2 + side, 64, stride=4)] = (
                        total[at:at + 64, r * 128:(r + 1) * 128]
                    )

    def z_start(kind, rho):
        i = held(kind, rho)
        for block in range(2):
            G[kind, rho, block] = G32[block].reshape(WAVES, 16, 128).astype(BF16)

        def block_to(block, to):
            there = (to, partner_col[kind] if block else col)
            send(G.at[kind, rho, block, to], F.at[i, w], there, z_send.at[kind, rho, block],
                 z_recv.at[i]).start()

        def one(k, _):
            d = 8 + (1 - 2 * lax.rem(k, 2)) * (k // 2)
            to = lax.rem(w + d, WAVES)
            block_to(1, to)
            block_to(0, to)
            return 0

        lax.fori_loop(1, WAVES, one, 0)
        block_to(1, w)
        F[i, w] = G[kind, rho, 0, w]

    def z_sent(kind, rho):
        for block in range(2):
            ref = F.at[0, pl.ds(0, WAVES - 1 + block)]
            bytes_of(ref, z_send.at[kind, rho, block], z_recv.at[0]).wait_send()

    def make_values(kind, rho, mine):
        i = held(kind, rho) if mine else given(kind, rho)
        ref = F.at[i, pl.ds(0, WAVES - 1 if mine else WAVES)]
        bytes_of(ref, z_send.at[kind, rho, 0], z_recv.at[i]).wait_recv()
        sign = SG[pl.ds(pl.multiple_of(i * 64, 64), 64)]
        tiles = F[i].astype(F32).reshape(8, 2, 2, 8, 128)
        top = iota((64, 128), 0) % 8 < 4
        for u2 in range(2):
            even = tiles[:, 0, u2].reshape(64, 128)
            odd = tiles[:, 1, u2].reshape(64, 128)
            swap_even = pltpu.roll(tiles[:, 0, u2], 4, 1).reshape(64, 128)
            swap_odd = pltpu.roll(tiles[:, 1, u2], 4, 1).reshape(64, 128)
            for u1 in range(2):
                part = jnp.where(top, even, swap_odd) if u1 == 0 else jnp.where(top, swap_even, odd)
                V[i, 2 * u2 + u1, :, 0:128] = part.astype(BF16)
                V[i, 2 * u2 + u1, :, 128:256] = (part * sign).astype(BF16)

    relay(0, 1)
    for kind in range(2):
        ln(kind, 1).start()
    lax.fori_loop(FIRST, SECOND, make_basis, 0)
    relay(1, 1)
    xe_all(1).wait_recv()
    n = jnp.zeros((1, 128), F32)
    for i in range(8):
        lo, _ = low_of(i)
        n = jnp.where(iota((1, 128), 1) == i, (1023 - lo).astype(F32), n)
    out = solve(XE[...].reshape(256, 128), 0, n, 128)
    for r in range(2):
        C[r * 128:(r + 1) * 128, 1024:1152] = out[r]
    for rho in range(ROUNDS):
        for kind in range(2):
            for part in range(2):
                p2_arrived(kind, rho, part, 1)
            ln(kind, rho).wait_recv()
            leg_spread(kind, rho, 128, RL.at[kind, rho])
            for part in range(2):
                p2_arrived(kind, rho, part, 2)
            field(kind, rho)
            z_start(kind, rho)

    lax.fori_loop(SECOND, 4, make_basis, 0)
    for rho in range(ROUNDS):
        for kind in range(2):
            make_values(kind, rho, True)
            make_values(kind, rho, False)
            if rho == 0 and kind == 0:
                for k in range(2):
                    for r in range(ROUNDS):
                        p1_all(k, r).wait_send()
                        ln(k, r).wait_send()
                        ref = X.at[k, r, pl.ds(0, 3)]
                        bytes_of(ref, p2_send.at[k, r], p2_recv.at[k, r, 0, 0]).wait_send()
                for stage in range(2):
                    xe_all(stage).wait_send()
    for kind in range(2):
        for rho in range(ROUNDS):
            z_sent(kind, rho)


def grid_kernel(cp_s, basis, V, out_hbm, D, PL, stage, out_sem):
    first = lax.axis_index("col") * 64 + lax.axis_index("wave") * 4

    def out_copy(u, b):
        at = pl.ds(b * 1024, 1024)
        return pltpu.make_async_copy(stage.at[u, at], out_hbm.at[0, u, at], out_sem.at[u, b])

    def sums(u):
        values = V[:, u].reshape(512, 256)
        k = u % 2
        for b in range(2):
            both = dot(basis[u, b * 1024:(b + 1) * 1024], values)
            D[k, 1024 + b * 1024:2048 + b * 1024] = both[:, 128:256]
            if b == 0:
                stage[u, 0:1024] = both[:, 0:128].astype(BF16)
            else:
                PL[k, 1024:2048] = both[:, 0:128]

    def place(u):
        points = cp_s[first + u]
        half = points >> 1
        k = u % 2
        def turned(at):
            return D[k, pl.ds(pl.multiple_of(1024 + at - half, 8), 256)]
        for q in range(4, 16):
            at = q * 256
            j = iota((256, 128), 0) + at
            if q < 8:
                value = jnp.where(j < half, PL[k, at:at + 256], turned(at))
            else:
                value = jnp.where(j < points, turned(at), 0.0)
            stage[u, at:at + 256] = value.astype(BF16)

    for u in range(5):
        if u < 4:
            sums(u)
        if u > 0:
            place(u - 1)
        if u < 4:
            out_copy(u, 0).start()
        if u > 0:
            for b in range(1, 4):
                out_copy(u - 1, b).start()
    for u in range(4):
        for b in range(4):
            out_copy(u, b).wait()


def on_device(divergence, analysis, synthesis, helmholtz, legendre, wavenumbers, cycle_points):
    vmem = pl.BlockSpec(memory_space=pltpu.VMEM)
    smem = pl.BlockSpec(memory_space=pltpu.SMEM)
    hbm = pl.BlockSpec(memory_space=pl.ANY)
    dma = pltpu.SemaphoreType.DMA
    basis, values = pl.pallas_call(
        gather_kernel,
        out_shape=(
            pltpu.VMEM((4, HALF, 512), BF16),
            pltpu.VMEM((PAIRS, 4, 64, 256), BF16),
        ),
        in_specs=[hbm] * 8,
        out_specs=(vmem, vmem),
        scratch_shapes=[
            pltpu.SMEM((256,), jnp.int32),
            pltpu.SMEM((1024,), jnp.int32),
            pltpu.VMEM((1, 256), jnp.int32),
            pltpu.VMEM((16, 2, 8, 1024), F32),
            pltpu.VMEM((128, 128), F32),
            pltpu.VMEM((128, 128), F32),
            pltpu.VMEM((1, 128), F32),
            pltpu.VMEM((2, ROUNDS, SIDE, SIDE, 2, 16, 512), BF16),
            pltpu.VMEM((2, ROUNDS, 2, 16, 512), BF16),
            pltpu.VMEM((SIDE, SIDE, 16, 128), BF16),
            pltpu.VMEM((16, 64, 1024), BF16),
            pltpu.VMEM((2, ROUNDS, 64, 1152), BF16),
            pltpu.VMEM((2, ROUNDS, 64, 1152), BF16),
            pltpu.VMEM((2, ROUNDS, 64, 1152), BF16),
            pltpu.VMEM((2, ROUNDS, 256, 1152), BF16),
            pltpu.VMEM((2, 512, 256), BF16),
            pltpu.VMEM((128, 256), BF16),
            pltpu.VMEM((128, 512), F32),
            pltpu.VMEM((256, 1152), BF16),
            pltpu.VMEM((2, 256, 128), F32),
            pltpu.VMEM((2, ROUNDS, 2, WAVES, 16, 128), BF16),
            pltpu.VMEM((PAIRS, WAVES, 16, 128), BF16),
            pltpu.VMEM((8, 512), F32),
            pltpu.VMEM((512, 128), F32),
            pltpu.VMEM((32, 512), F32),
            pltpu.VMEM((32, 512), F32),
            pltpu.VMEM((64, 512), F32),
            pltpu.VMEM((64, 512), F32),
            dma((2, ROUNDS)), dma((2, ROUNDS)),
            dma((2, ROUNDS)), dma((2, ROUNDS, 2, 3)),
            dma((2,)), dma((2,)),
            dma((2, ROUNDS)), dma((2, ROUNDS)),
            dma((2, ROUNDS, 2)), dma((PAIRS,)),
            dma(()), dma((7,)),
        ],
        compiler_params=pltpu.CompilerParams(
            collective_id=0, has_side_effects=True, vmem_limit_bytes=50 * MIB
        ),
        cost_estimate=pl.CostEstimate(flops=4 << 30, bytes_accessed=12 * MIB, transcendentals=0),
    )(
        wavenumbers, cycle_points, wavenumbers.reshape(1, 256), divergence, analysis, synthesis,
        helmholtz.reshape(1, 128), jnp.swapaxes(legendre, 1, 2),
    )
    return pl.pallas_call(
        grid_kernel,
        out_shape=jax.ShapeDtypeStruct((1, 4, LON, 128), BF16),
        in_specs=[smem, vmem, vmem],
        out_specs=hbm,
        scratch_shapes=[
            pltpu.VMEM((2, LON, 128), F32),
            pltpu.VMEM((2, HALF, 128), F32),
            pltpu.VMEM((4, LON, 128), BF16),
            dma((4, 4)),
        ],
        compiler_params=pltpu.CompilerParams(vmem_limit_bytes=30 * MIB),
        cost_estimate=pl.CostEstimate(flops=4 << 30, bytes_accessed=13 * MIB, transcendentals=0),
    )(cycle_points, basis, values)


def solution(mesh):
    placed = (P("wave", None, "col", None), P(), P(), P(), P("wave", None, "col"), P(), P())
    return jax.shard_map(
        on_device,
        mesh=mesh,
        in_specs=placed,
        out_specs=P("col", "wave", None, None),
        check_vma=False,
    )
```

```python
import math

import jax
import jax.numpy as jnp
from jax import lax
from jax.experimental import pallas as pl
from jax.experimental.pallas import tpu as pltpu
from jax.sharding import PartitionSpec as P

MESH = pl.DeviceIdType.MESH
F32 = jnp.float32
BF16 = jnp.bfloat16
LON = 4096
WAVES = 16
HALF = LON // 2
SIDE = 4
ROUNDS = 2
PAIRS = 8
FIRST, SECOND = 0, 1
MIB = 1 << 20


def iota(shape, dim):
    return lax.broadcasted_iota(jnp.int32, shape, dim)


def dot(a, b):
    return jnp.dot(a, b, preferred_element_type=F32)


def cos_sin(turn):
    quadrant = jnp.floor(turn + 0.5)
    x = (turn - quadrant) * (0.5 * math.pi)
    z = x * x
    s = x * (1.0 + z * (-1.0 / 6 + z * (1.0 / 120 + z * (-1.0 / 5040 + z * (1.0 / 362880)))))
    c = 1.0 + z * (-0.5 + z * (1.0 / 24 + z * (-1.0 / 720 + z * (1.0 / 40320))))
    odd = (quadrant == 1.0) | (quadrant == 3.0)
    cosine = jnp.where(odd, s, c)
    sine = jnp.where(odd, c, s)
    cosine = jnp.where((quadrant == 1.0) | (quadrant == 2.0), -cosine, cosine)
    sine = jnp.where((quadrant == 2.0) | (quadrant == 3.0), -sine, sine)
    return cosine, sine


def gather_kernel(
    wn_hbm, cp_hbm, wn_row, div_hbm, analysis_hbm, synthesis_hbm, helm_hbm, leg_hbm, basis, V,
    wn_s, cp_s, wn_v, div, analysis, synthesis, helm,
    X, N, XE, leg, OL, LN, RL, LP, AHL, SS, HM, C, G32, G, F, ML, SG, UA, VA, CB, SB,
    p1_send, p1_recv, p2_send, p2_recv, xe_send, xe_recv, ln_send, ln_recv, z_send, z_recv,
    leg_sem, in_sem,
):
    w = lax.axis_index("wave")
    col = lax.axis_index("col")
    cx, cy = col // SIDE, col % SIDE

    def wrap(v, n=SIDE):
        return lax.rem(v + n, n)

    first = (cx, cy)
    second = (cy, cx)

    def toward(d):
        by = 1 - 2 * (d % 2)
        return by, -by

    def held(kind, rho):
        return kind * 4 + 2 * rho + ((first[kind] + 1) // 2) % 2

    def given(kind, rho):
        return kind * 4 + 2 * rho + 1 - ((first[kind] + 1) // 2) % 2

    def column(kind, d1, d2):
        return d1 * SIDE + d2 if kind == 0 else d2 * SIDE + d1

    def step_first(kind, by):
        return (w, column(kind, wrap(first[kind] + by), second[kind]))

    def step_second(kind, by):
        return (w, column(kind, first[kind], wrap(second[kind] + by)))

    fetches = [
        pltpu.make_async_copy(src, dst, in_sem.at[k])
        for k, (src, dst) in enumerate((
            (wn_hbm, wn_s), (div_hbm, div), (cp_hbm, cp_s), (wn_row, wn_v),
            (analysis_hbm, analysis), (synthesis_hbm, synthesis), (helm_hbm, helm),
        ))
    ]
    for fetch in fetches:
        fetch.start()
    barrier = pltpu.get_barrier_semaphore()
    for kind in range(2):
        for by in (1, 2, 3):
            pl.semaphore_signal(barrier, inc=1, device_id=step_first(kind, by), device_id_type=MESH)

    partner_col = [step_first(kind, toward(first[kind])[0])[1] for kind in range(2)]

    def greet(d, _):
        for to in (col, partner_col[0], partner_col[1]):
            pl.semaphore_signal(
                barrier, inc=1, device_id=(lax.rem(w + d, WAVES), to), device_id_type=MESH
            )
        return 0

    lax.fori_loop(1, WAVES, greet, 0)
    leg_copy = pltpu.make_async_copy(leg_hbm, leg, leg_sem)
    leg_copy.start()

    def low_of(i):
        m = wn_s[w * 16 + 2 * i]
        return jnp.minimum(m, 1023 - m), jnp.where(m > 511, 1, 0)

    for fetch in fetches:
        fetch.wait()

    lanes = iota((16, 512), 1)
    tile_lane = iota((16, 128), 1)
    extra = jnp.zeros((16, 128), F32)
    for kind in range(2):
        for rho in range(ROUNDS):
            for keep in range(2):
                i = held(kind, rho) if keep else given(kind, rho)
                lo, swap = low_of(i)
                low = div[2 * i + swap].reshape(16, 1024)
                high = div[2 * i + 1 - swap].reshape(16, 1024)
                rolled = pltpu.roll(high[:, 512:], lo, 1)
                own = X.at[kind, rho, second[kind], 0] if keep else N.at[kind, rho]
                own[0] = jnp.where(lanes >= lo, low[:, :512], rolled).astype(BF16)
                own[1] = low[:, 512:].astype(BF16)
                moved = pltpu.roll(rolled[:, 384:], i + 1, 1)
                extra = jnp.where(tile_lane == i, moved, extra)
    XE[cy, 0] = extra.astype(BF16)

    def make_angles(u):
        latitude = col * 64 + w * 4 + u

        def angle(index, count):
            points = jnp.full((count, 512), cp_s[latitude], jnp.int32).astype(F32)
            inverse = 1.0 / points
            product = index.astype(F32) * jnp.broadcast_to(ML[0:1], (count, 512))
            rest = product - jnp.floor(product * inverse) * points
            rest = jnp.where(rest < 0.0, rest + points, rest)
            rest = jnp.where(rest >= points, rest - points, rest)
            return cos_sin(rest * (4.0 * inverse))

        c, s = angle(iota((32, 512), 0) * 64, 32)
        weight = jnp.where(ML[0:1] == 0.0, 1.0, 2.0) / math.sqrt(256.0)
        imaginary = ((iota((32, 512), 1) >> 1) & 1) == 1
        c, s = weight * c, -weight * s
        UA[...] = jnp.where(imaginary, s, c)
        VA[...] = jnp.where(imaginary, -c, s)
        c, s = angle(iota((64, 512), 0), 64)
        CB[...] = c
        SB[...] = s

    def make_basis(u, _):
        make_angles(u)

        def rows(a8, _):
            some = pl.ds(pl.multiple_of(a8 * 8, 8), 8)
            for q in range(4):
                at = pl.ds(q * 128, 128)
                ua, va, cb, sb = UA[some, at], VA[some, at], CB[:, at], SB[:, at]
                for k in range(8):
                    value = ua[k:k + 1] * cb + va[k:k + 1] * sb
                    start = pl.multiple_of(a8 * 512, 512) + k * 64
                    basis[u, pl.ds(start, 64), at] = value.astype(BF16)
            return 0

        lax.fori_loop(0, HALF // 512, rows, 0)
        return 0

    def leg_pack(i, to):
        lo, swap = low_of(i)
        low = leg.at[2 * i + swap]
        high = leg.at[2 * i + 1 - swap]
        rolled = pltpu.roll(high[:, 512:].astype(F32), lo, 1)
        both = jnp.where(iota((64, 512), 1) >= lo, low[:, 0:512].astype(F32), rolled)
        to[:, 0:512] = both.astype(BF16)
        to[:, 512:1024] = low[:, 512:]
        moved = pltpu.roll(rolled[:, 384:], i + 1, 1)
        to[:, 1024:1152] = jnp.where(iota((64, 128), 1) == i, moved, 0.0).astype(BF16)

    def leg_spread(kind, rho, at, block):
        lo, _ = low_of(held(kind, rho))
        p = iota((64, 512), 1)
        both = block[:, 0:512].astype(F32)
        to = LP.at[kind, rho]
        to[at:at + 64, 0:512] = jnp.where(p >= lo, both, 0.0).astype(BF16)
        to[at + 64:at + 128, 0:512] = jnp.where(p < lo, both, 0.0).astype(BF16)
        to[at:at + 64, 512:1024] = block[:, 512:1024]
        to[at + 64:at + 128, 512:1024] = jnp.zeros((64, 512), BF16)
        to[at:at + 64, 1024:1152] = jnp.zeros((64, 128), BF16)
        to[at + 64:at + 128, 1024:1152] = block[:, 1024:1152]

    pl.semaphore_wait(barrier, 6 + 3 * (WAVES - 1))

    def send(src, dst, to, send_sem, recv_sem):
        return pltpu.make_async_remote_copy(
            src_ref=src, dst_ref=dst, send_sem=send_sem, recv_sem=recv_sem,
            device_id=to, device_id_type=MESH,
        )

    def bytes_of(ref, send_sem, recv_sem):
        return send(ref, ref, step_first(0, 1), send_sem, recv_sem)

    def p1_start(kind, rho):
        own = X.at[kind, rho, second[kind], 0]
        partner, other = toward(first[kind])
        for src, by in ((N.at[kind, rho], 2), (N.at[kind, rho], partner), (own, other)):
            to = X.at[kind, rho, second[kind], wrap(-by)]
            send(src, to, step_first(kind, by), p1_send.at[kind, rho], p1_recv.at[kind, rho]).start()

    def p1_all(kind, rho):
        ref = X.at[kind, rho, second[kind], pl.ds(0, 3)]
        return bytes_of(ref, p1_send.at[kind, rho], p1_recv.at[kind, rho])

    def p2(kind, rho, part, which):
        d2 = second[kind]
        partner, other = toward(d2)
        row = wrap(d2 + partner) if which == 2 else d2
        ref = X.at[kind, rho, row, pl.ds(0, 1) if part == 0 else pl.ds(1, 3)]
        to = step_second(kind, partner if which == 0 else other)
        return send(ref, ref, to, p2_send.at[kind, rho], p2_recv.at[kind, rho, part, which])

    def p2_direct(rho, part):
        for which in range(2):
            for kind in range(2):
                p2(kind, rho, part, which).start()

    def p2_arrived(kind, rho, part, which):
        partner, other = toward(second[kind])
        row = wrap(second[kind] + (partner, other, 2)[which])
        ref = X.at[kind, rho, row, pl.ds(0, 1) if part == 0 else pl.ds(1, 3)]
        bytes_of(ref, p2_send.at[kind, rho], p2_recv.at[kind, rho, part, which]).wait_recv()

    def ln(kind, rho):
        to = step_first(kind, toward(first[kind])[0])
        return send(LN.at[kind, rho], RL.at[kind, rho], to, ln_send.at[kind, rho], ln_recv.at[kind, rho])

    def relay(rho, part):
        for kind in range(2):
            p2_arrived(kind, rho, part, 0)
            p2(kind, rho, part, 2).start()

    def xe_start(stage):
        for by in (2, 1, 3):
            src = XE.at[cy, 0] if stage == 0 else XE.at[cy]
            dst = XE.at[cy, 4 - by] if stage == 0 else XE.at[cy]
            to = step_first(0, by) if stage == 0 else step_second(0, by)
            send(src, dst, to, xe_send.at[stage], xe_recv.at[stage]).start()

    def xe_all(stage):
        ref = XE.at[cy, pl.ds(0, 3)] if stage == 0 else XE.at[pl.ds(0, 3)]
        return bytes_of(ref, xe_send.at[stage], xe_recv.at[stage])

    for rho in range(ROUNDS):
        for kind in range(2):
            p1_start(kind, rho)
        if rho == 0:
            xe_start(0)
    for rho in range(ROUNDS):
        p2_direct(rho, 0)

    leg_copy.wait()
    for rho in range(ROUNDS):
        for kind in range(2):
            leg_pack(given(kind, rho), LN.at[kind, rho])
    for rho in range(ROUNDS):
        for kind in range(2):
            p1_all(kind, rho).wait_recv()
        if rho == 0:
            xe_all(0).wait_recv()
            xe_start(1)
        p2_direct(rho, 1)
        if rho == 0:
            for kind in range(2):
                ln(kind, 0).start()
    for rho in range(ROUNDS):
        relay(rho, 0)
    for kind in range(2):
        ln(kind, 1).start()
    a_full = analysis[...]
    a_hi = a_full.astype(BF16)
    a_lo = (a_full - a_hi.astype(F32)).astype(BF16)
    row = iota((128, 256), 0)
    j = iota((128, 256), 1)
    j2, j1 = j >> 6, (j >> 4) & 3
    for kind in range(2):
        j_first = (j1 + first[kind]) & 3
        level = column(kind, j_first, j2) * 8 + (j & 7)
        for r in range(2):
            pick = jnp.where((row == level) & (((j >> 3) & 1) == r), 1.0, 0.0).astype(BF16)
            AHL[kind, r * 128:(r + 1) * 128] = dot(a_hi, pick).astype(BF16)
            AHL[kind, 256 + r * 128:256 + (r + 1) * 128] = dot(a_lo, pick).astype(BF16)
    s_full = synthesis[...]
    s_hi = s_full.astype(BF16)
    SS[:, 0:128] = s_hi
    SS[:, 128:256] = (s_full - s_hi.astype(F32)).astype(BF16)
    h_rows = jnp.broadcast_to(helm[...], (128, 128)).T
    for q in range(4):
        HM[:, q * 128:(q + 1) * 128] = h_rows

    lane = iota((256, 512), 1)
    slot = ((lane >> 2) & 15) * 16 + 2 * (lane >> 6)
    choose = jnp.where(iota((256, 512), 0) == slot, 1.0, 0.0).astype(BF16)
    wn = jnp.broadcast_to(wn_v[...], (16, 256))
    upper = dot((wn >> 5).astype(F32).astype(BF16), choose)
    lower = dot((wn & 31).astype(F32).astype(BF16), choose)
    m0 = (upper * 32.0 + lower)[0:8]
    m_lo = jnp.minimum(m0, 1023.0 - m0)
    m_lane = jnp.where((iota((8, 512), 1) & 1) == 1, 1023.0 - m_lo, m_lo)
    ML[...] = m_lane
    sign = 1.0 - 2.0 * (m_lane - 2.0 * jnp.floor(m_lane * 0.5))
    for q in range(4):
        part = jnp.broadcast_to(sign[0:1, q * 128:(q + 1) * 128], (128, 128))
        SG[q * 128:(q + 1) * 128] = part.T

    for rho in range(ROUNDS):
        for kind in range(2):
            leg_pack(held(kind, rho), OL.at[kind, rho])
            leg_spread(kind, rho, 0, OL.at[kind, rho])
    lax.fori_loop(0, FIRST, make_basis, 0)

    def solve(x, kind, n, count):
        modes = dot(AHL[kind], x)
        modes = modes[0:256] + modes[256:512]
        factor = 1.0 / (1.0 + HM[:, 0:count] * (n * (n + 1.0)))
        out = []
        for r in range(2):
            part = modes[r * 128:(r + 1) * 128] * factor
            hi = part.astype(BF16)
            lo = (part - hi.astype(F32)).astype(BF16)
            both = jnp.concatenate([hi, hi], axis=0)
            out.append((dot(SS[...], both) + dot(SS[:, 0:128], lo)).astype(BF16))
        return out

    def field(kind, rho):
        lo, _ = low_of(held(kind, rho))
        for h in range(2):
            p = iota((1, 512), 1) + h * 512
            n = jnp.where(p >= lo, p, p + 1024 - lo).astype(F32)
            x = X[kind, rho, :, :, h].reshape(256, 512)
            out = solve(x, kind, n, 512)
            for r in range(2):
                C[r * 128:(r + 1) * 128, h * 512:(h + 1) * 512] = out[r]
        table = LP.at[kind, rho]
        contract = (((1,), (1,)), ((), ()))
        total = lax.dot_general(table[...], C[...], contract, preferred_element_type=F32)
        for block in range(2):
            for side in range(2):
                for r in range(2):
                    at = block * 128 + side * 64
                    G32[block, pl.ds(r * 2 + side, 64, stride=4)] = (
                        total[at:at + 64, r * 128:(r + 1) * 128]
                    )

    def z_start(kind, rho):
        i = held(kind, rho)
        for block in range(2):
            G[kind, rho, block] = G32[block].reshape(WAVES, 16, 128).astype(BF16)

        def block_to(block, to):
            there = (to, partner_col[kind] if block else col)
            send(G.at[kind, rho, block, to], F.at[i, w], there, z_send.at[kind, rho, block],
                 z_recv.at[i]).start()

        def one(k, _):
            d = 8 + (1 - 2 * lax.rem(k, 2)) * (k // 2)
            to = lax.rem(w + d, WAVES)
            block_to(1, to)
            block_to(0, to)
            return 0

        lax.fori_loop(1, WAVES, one, 0)
        block_to(1, w)
        F[i, w] = G[kind, rho, 0, w]

    def z_sent(kind, rho):
        for block in range(2):
            ref = F.at[0, pl.ds(0, WAVES - 1 + block)]
            bytes_of(ref, z_send.at[kind, rho, block], z_recv.at[0]).wait_send()

    def make_values(kind, rho, mine):
        i = held(kind, rho) if mine else given(kind, rho)
        ref = F.at[i, pl.ds(0, WAVES - 1 if mine else WAVES)]
        bytes_of(ref, z_send.at[kind, rho, 0], z_recv.at[i]).wait_recv()
        sign = SG[pl.ds(pl.multiple_of(i * 64, 64), 64)]
        tiles = F[i].astype(F32).reshape(8, 2, 2, 8, 128)
        top = iota((64, 128), 0) % 8 < 4
        for u2 in range(2):
            even = tiles[:, 0, u2].reshape(64, 128)
            odd = tiles[:, 1, u2].reshape(64, 128)
            swap_even = pltpu.roll(tiles[:, 0, u2], 4, 1).reshape(64, 128)
            swap_odd = pltpu.roll(tiles[:, 1, u2], 4, 1).reshape(64, 128)
            for u1 in range(2):
                part = jnp.where(top, even, swap_odd) if u1 == 0 else jnp.where(top, swap_even, odd)
                V[i, 2 * u2 + u1, :, 0:128] = part.astype(BF16)
                V[i, 2 * u2 + u1, :, 128:256] = (part * sign).astype(BF16)

    relay(0, 1)
    lax.fori_loop(FIRST, SECOND, make_basis, 0)
    relay(1, 1)
    xe_all(1).wait_recv()
    n = jnp.zeros((1, 128), F32)
    for i in range(8):
        lo, _ = low_of(i)
        n = jnp.where(iota((1, 128), 1) == i, (1023 - lo).astype(F32), n)
    out = solve(XE[...].reshape(256, 128), 0, n, 128)
    for r in range(2):
        C[r * 128:(r + 1) * 128, 1024:1152] = out[r]
    for rho in range(ROUNDS):
        for kind in range(2):
            for part in range(2):
                p2_arrived(kind, rho, part, 1)
            ln(kind, rho).wait_recv()
            leg_spread(kind, rho, 128, RL.at[kind, rho])
            for part in range(2):
                p2_arrived(kind, rho, part, 2)
            field(kind, rho)
            z_start(kind, rho)

    lax.fori_loop(SECOND, 4, make_basis, 0)
    for rho in range(ROUNDS):
        for kind in range(2):
            make_values(kind, rho, True)
            make_values(kind, rho, False)
            if rho == 0 and kind == 0:
                for k in range(2):
                    for r in range(ROUNDS):
                        p1_all(k, r).wait_send()
                        ln(k, r).wait_send()
                        ref = X.at[k, r, pl.ds(0, 3)]
                        bytes_of(ref, p2_send.at[k, r], p2_recv.at[k, r, 0, 0]).wait_send()
                for stage in range(2):
                    xe_all(stage).wait_send()
    for kind in range(2):
        for rho in range(ROUNDS):
            z_sent(kind, rho)


def grid_kernel(cp_s, basis, V, out_hbm, D, PL, stage, out_sem):
    first = lax.axis_index("col") * 64 + lax.axis_index("wave") * 4

    def out_copy(u, b):
        at = pl.ds(b * 1024, 1024)
        return pltpu.make_async_copy(stage.at[u, at], out_hbm.at[0, u, at], out_sem.at[u, b])

    def sums(u):
        values = V[:, u].reshape(512, 256)
        k = u % 2
        for b in range(2):
            both = dot(basis[u, b * 1024:(b + 1) * 1024], values)
            D[k, 1024 + b * 1024:2048 + b * 1024] = both[:, 128:256]
            if b == 0:
                stage[u, 0:1024] = both[:, 0:128].astype(BF16)
            else:
                PL[k, 1024:2048] = both[:, 0:128]

    def place(u):
        points = cp_s[first + u]
        half = points >> 1
        k = u % 2
        def turned(at):
            return D[k, pl.ds(pl.multiple_of(1024 + at - half, 8), 256)]
        for q in range(4, 16):
            at = q * 256
            j = iota((256, 128), 0) + at
            if q < 8:
                value = jnp.where(j < half, PL[k, at:at + 256], turned(at))
            else:
                value = jnp.where(j < points, turned(at), 0.0)
            stage[u, at:at + 256] = value.astype(BF16)

    for u in range(5):
        if u < 4:
            sums(u)
        if u > 0:
            place(u - 1)
        if u < 4:
            out_copy(u, 0).start()
        if u > 0:
            for b in range(1, 4):
                out_copy(u - 1, b).start()
    for u in range(4):
        for b in range(4):
            out_copy(u, b).wait()


def on_device(divergence, analysis, synthesis, helmholtz, legendre, wavenumbers, cycle_points):
    vmem = pl.BlockSpec(memory_space=pltpu.VMEM)
    smem = pl.BlockSpec(memory_space=pltpu.SMEM)
    hbm = pl.BlockSpec(memory_space=pl.ANY)
    dma = pltpu.SemaphoreType.DMA
    basis, values = pl.pallas_call(
        gather_kernel,
        out_shape=(
            pltpu.VMEM((4, HALF, 512), BF16),
            pltpu.VMEM((PAIRS, 4, 64, 256), BF16),
        ),
        in_specs=[hbm] * 8,
        out_specs=(vmem, vmem),
        scratch_shapes=[
            pltpu.SMEM((256,), jnp.int32),
            pltpu.SMEM((1024,), jnp.int32),
            pltpu.VMEM((1, 256), jnp.int32),
            pltpu.VMEM((16, 2, 8, 1024), F32),
            pltpu.VMEM((128, 128), F32),
            pltpu.VMEM((128, 128), F32),
            pltpu.VMEM((1, 128), F32),
            pltpu.VMEM((2, ROUNDS, SIDE, SIDE, 2, 16, 512), BF16),
            pltpu.VMEM((2, ROUNDS, 2, 16, 512), BF16),
            pltpu.VMEM((SIDE, SIDE, 16, 128), BF16),
            pltpu.VMEM((16, 64, 1024), BF16),
            pltpu.VMEM((2, ROUNDS, 64, 1152), BF16),
            pltpu.VMEM((2, ROUNDS, 64, 1152), BF16),
            pltpu.VMEM((2, ROUNDS, 64, 1152), BF16),
            pltpu.VMEM((2, ROUNDS, 256, 1152), BF16),
            pltpu.VMEM((2, 512, 256), BF16),
            pltpu.VMEM((128, 256), BF16),
            pltpu.VMEM((128, 512), F32),
            pltpu.VMEM((256, 1152), BF16),
            pltpu.VMEM((2, 256, 128), F32),
            pltpu.VMEM((2, ROUNDS, 2, WAVES, 16, 128), BF16),
            pltpu.VMEM((PAIRS, WAVES, 16, 128), BF16),
            pltpu.VMEM((8, 512), F32),
            pltpu.VMEM((512, 128), F32),
            pltpu.VMEM((32, 512), F32),
            pltpu.VMEM((32, 512), F32),
            pltpu.VMEM((64, 512), F32),
            pltpu.VMEM((64, 512), F32),
            dma((2, ROUNDS)), dma((2, ROUNDS)),
            dma((2, ROUNDS)), dma((2, ROUNDS, 2, 3)),
            dma((2,)), dma((2,)),
            dma((2, ROUNDS)), dma((2, ROUNDS)),
            dma((2, ROUNDS, 2)), dma((PAIRS,)),
            dma(()), dma((7,)),
        ],
        compiler_params=pltpu.CompilerParams(
            collective_id=0, has_side_effects=True, vmem_limit_bytes=50 * MIB
        ),
        cost_estimate=pl.CostEstimate(flops=4 << 30, bytes_accessed=12 * MIB, transcendentals=0),
    )(
        wavenumbers, cycle_points, wavenumbers.reshape(1, 256), divergence, analysis, synthesis,
        helmholtz.reshape(1, 128), jnp.swapaxes(legendre, 1, 2),
    )
    return pl.pallas_call(
        grid_kernel,
        out_shape=jax.ShapeDtypeStruct((1, 4, LON, 128), BF16),
        in_specs=[smem, vmem, vmem],
        out_specs=hbm,
        scratch_shapes=[
            pltpu.VMEM((2, LON, 128), F32),
            pltpu.VMEM((2, HALF, 128), F32),
            pltpu.VMEM((4, LON, 128), BF16),
            dma((4, 4)),
        ],
        compiler_params=pltpu.CompilerParams(vmem_limit_bytes=30 * MIB),
        cost_estimate=pl.CostEstimate(flops=4 << 30, bytes_accessed=13 * MIB, transcendentals=0),
    )(cycle_points, basis, values)


def solution(mesh):
    placed = (P("wave", None, "col", None), P(), P(), P(), P("wave", None, "col"), P(), P())
    return jax.shard_map(
        on_device,
        mesh=mesh,
        in_specs=placed,
        out_specs=P("col", "wave", None, None),
        check_vma=False,
    )
```
